32 devices in a mesh: groups: 2 (over y), beam: 4 (over x, core), tile: 4 (over z).
Axes of the slice: x: 2, y: 2, z: 4, core: 2. Of those that a mesh axis runs over, the one named last changes fastest.
Arguments:
- smatrix: bfloat16 [2, 512, 512, 128], P(None, ('groups', 'beam'), 'tile'), parts along dimension 1, may hold values from -6 to 6
- beam_table: float32 [3, 256], P(None, 'beam'), may hold values from -8 to 8
- probes: int32 [64, 2], P(('groups', 'tile')), parts along dimension 0, may hold values from 0 to 2047, as said below
Outputs:
- diffraction: float32 [64, 32, 32], P(('groups', 'tile'), 'beam'), parts along dimension 0
The draws below stay inside these ranges and needn't reach their ends.
There are 2 independent parts, one for each index of `groups`. The reference program is written for one: setup_inputs(seed, part) draws one part's arguments, and reference() takes and returns one part's arrays. A program takes and returns all parts, laid end to end along the dimension named above; an argument that names none is the same for every part. Nothing has to cross between parts.
Inputs may be any that keep to these rules, and one draw needn't show every extreme that they name: A probe's window starts at reduced row (row // 4 - 128 // 2) mod 512; the block of 128 rows holding that start is its window tile. Among the 8 probes of one index of tile at most 2 have the same window tile, and in every draw one window tile has exactly 2 probes from every index of tile. Columns lie below 512.
All inputs are finite; a program needn't handle non-finite values.
Results may differ from the reference program's by a relative error of at most 0.01.
Values may be sent and summed in bfloat16 or wider, within the bound.
No kernel may reach another device: no remote copies, remote signals or barrier semaphores. Data moves between devices by JAX's collectives and lax.ppermute only.
A program may use at most 64 MiB of HBM per device.

```python
import math
import jax
import jax.numpy as jnp
from jax import lax

W = 128
K = 64
IF = 4
BIN = 2
B_DEV = 64
BEAMS = 256
FY = 512
PROBE_DEV = 8
PROBES = 32
N_BEAM = 4
N_TILE = 4


def draw_probes(key, part):
    key = jax.random.fold_in(key, 7)
    subkeys = jax.random.split(key, 7)
    per_tile = PROBE_DEV // 4
    spread_count = PROBE_DEV - per_tile
    hot_tile = jax.random.randint(subkeys[0], (), 0, N_TILE)
    owner_bias = jax.random.randint(subkeys[1], (N_TILE,), 0, 4)
    tokens = N_TILE * per_tile
    token_tile = jnp.arange(tokens, dtype=jnp.int32) // per_tile
    scores = jax.random.randint(subkeys[2], (N_TILE, tokens), 0, 256) + 256 * owner_bias[token_tile][None, :]
    scores = jnp.where(token_tile[None, :] == hot_tile, -1, scores)
    scores = scores * tokens + jnp.arange(tokens, dtype=jnp.int32)[None, :]
    ranked = jnp.argsort(-scores, axis=1)
    chosen = token_tile[ranked[:, :spread_count]]
    owners = jnp.concatenate([jnp.full((N_TILE, per_tile), hot_tile, jnp.int32), chosen.astype(jnp.int32)], axis=1)
    shuffle_keys = jax.random.randint(subkeys[3], (N_TILE, PROBE_DEV), 0, 1 << 20) * PROBE_DEV + jnp.arange(PROBE_DEV, dtype=jnp.int32)[None, :]
    shuffle = jnp.argsort(shuffle_keys, axis=1)
    owners = jnp.take_along_axis(owners, shuffle, axis=1).reshape(-1)
    field_rows = W * N_TILE
    offset = jax.random.randint(subkeys[4], (PROBES,), 0, W)
    sub_row = jax.random.randint(subkeys[5], (PROBES,), 0, IF)
    column = jax.random.randint(subkeys[6], (PROBES,), 0, W * IF)
    start_row = owners * W + offset
    fine_row = jnp.mod(start_row + W // 2, field_rows) * IF + sub_row
    return jnp.stack([fine_row, column], axis=1).astype(jnp.int32)


def block_scale(key, extent, shards, smallest, largest):
    def one(position, parts):
        heights = jax.random.uniform(jax.random.fold_in(jax.random.fold_in(key, 6), position), (parts,), jnp.float32, smallest / len(shards), largest / len(shards))
        return jnp.repeat(jnp.exp(heights), extent[position] // parts).reshape((-1,) + (1,) * (len(extent) - position - 1))

    factor_of = one(*shards[0])
    for cut in shards[1:]:
        factor_of = factor_of * one(*cut)
    return factor_of


def gaussian(key, extent, scale, limit, cuts=(), kind=jnp.bfloat16):
    drawn = scale * jax.random.normal(key, extent, jnp.float32)
    if cuts:
        drawn = drawn * block_scale(key, extent, cuts, -0.22, 0.18)
    return jnp.clip(drawn, -limit, limit).astype(kind)


def setup_inputs(seed: int = 0, part: int = 0) -> dict:
    key_of = jax.random.split(jax.random.key(seed), 4)
    own_keys = jax.random.split(jax.random.fold_in(key_of[3], part), 4)
    return {
        "smatrix": gaussian(own_keys[0], (2, BEAMS, FY, W), 1.0, 6.0, ((1, 4), (2, 4))),
        "beam_table": jnp.clip(jax.random.uniform(key_of[1], (3, BEAMS), jnp.float32, -8.0, 8.0) * block_scale(key_of[1], (3, BEAMS), ((1, 4),), -0.4, 0.0), -8.0, 8.0),
        "probes": draw_probes(jax.random.fold_in(jax.random.fold_in(key_of[3], part), 71), part),
    }


two_pi = 2.0 * math.pi


def dft_tables(window, kept_freq):
    column_idx = jnp.arange(window, dtype=jnp.int32)
    v_freq = jnp.arange(kept_freq, dtype=jnp.int32) - kept_freq // 2
    angle_v = (two_pi / window) * jnp.mod(column_idx[:, None] * v_freq[None, :], window).astype(jnp.float32)
    return jnp.cos(angle_v).astype(jnp.bfloat16), jnp.sin(angle_v).astype(jnp.bfloat16)


def rounded(values):
    return lax.optimization_barrier(values.astype(jnp.bfloat16)).astype(jnp.float32)


def reference(smatrix, beam_table, probes):
    table_cos, table_sin = dft_tables(W, K)

    def group_spectra(group):
        piece = lax.dynamic_slice_in_dim(smatrix, group * B_DEV, B_DEV, 1)
        real_rows = piece[0].reshape(-1, W)
        imag_rows = piece[1].reshape(-1, W)
        out_re = jnp.dot(real_rows, table_cos, preferred_element_type=jnp.float32) + jnp.dot(imag_rows, table_sin, preferred_element_type=jnp.float32)
        out_im = jnp.dot(imag_rows, table_cos, preferred_element_type=jnp.float32) - jnp.dot(real_rows, table_sin, preferred_element_type=jnp.float32)
        return jnp.stack([out_re, out_im]).astype(jnp.bfloat16).reshape(2, B_DEV, FY, K)

    spectra = lax.map(group_spectra, jnp.arange(N_BEAM, dtype=jnp.int32))
    block_size = 2

    def probe_block(places):
        pos_row = places[:, 0]
        pos_col = places[:, 1]
        start_row = jnp.mod(pos_row // IF - W // 2, FY)
        owner_tile = start_row // W
        offset = jnp.mod(start_row, W)
        shift_x = jnp.mod(pos_col // IF - W // 2, W)
        row_ids = jnp.mod(owner_tile[:, None] * W + jnp.arange(2 * W, dtype=jnp.int32)[None, :], FY)
        selected = jnp.take(spectra, row_ids.reshape(-1), axis=3).reshape(N_BEAM, 2, B_DEV, block_size, 2 * W, K)
        sel_re = selected[:, 0].astype(jnp.float32)
        sel_im = selected[:, 1].astype(jnp.float32)
        phase = beam_table[2][None, :] + (two_pi / (W * IF)) * (beam_table[0][None, :] * pos_row[:, None].astype(jnp.float32) + beam_table[1][None, :] * pos_col[:, None].astype(jnp.float32))
        alpha_re = rounded(jnp.cos(phase)).reshape(block_size, N_BEAM, B_DEV)
        alpha_im = rounded(-jnp.sin(phase)).reshape(block_size, N_BEAM, B_DEV)
        wave_re = jnp.einsum('pgb,gbprv->gprv', alpha_re, sel_re) - jnp.einsum('pgb,gbprv->gprv', alpha_im, sel_im)
        wave_im = jnp.einsum('pgb,gbprv->gprv', alpha_im, sel_re) + jnp.einsum('pgb,gbprv->gprv', alpha_re, sel_im)
        wave_re = rounded(wave_re)
        wave_im = rounded(wave_im)
        u_freq = jnp.arange(K, dtype=jnp.int32) - K // 2
        row_pos = jnp.arange(2 * W, dtype=jnp.int32)[None, None, :] - offset[:, None, None]
        inside = (row_pos >= 0) & (row_pos < W)
        angle_u = (-two_pi / W) * jnp.mod(u_freq[None, :, None] * row_pos, W).astype(jnp.float32)
        kern_re = rounded(jnp.where(inside, jnp.cos(angle_u), 0.0))
        kern_im = rounded(jnp.where(inside, jnp.sin(angle_u), 0.0))
        out_re = jnp.einsum('pur,gprv->gpuv', kern_re, wave_re) - jnp.einsum('pur,gprv->gpuv', kern_im, wave_im)
        out_im = jnp.einsum('pur,gprv->gpuv', kern_re, wave_im) + jnp.einsum('pur,gprv->gpuv', kern_im, wave_re)
        v_freq = jnp.arange(K, dtype=jnp.int32) - K // 2
        turn = (two_pi / W) * jnp.mod(v_freq[None, :] * shift_x[:, None], W).astype(jnp.float32)
        cos_turn = jnp.cos(turn)[None, :, None, :]
        sin_turn = jnp.sin(turn)[None, :, None, :]
        part_re = rounded(out_re * cos_turn - out_im * sin_turn)
        part_im = rounded(out_re * sin_turn + out_im * cos_turn)
        field_re = jnp.sum(part_re, axis=0)
        field_im = jnp.sum(part_im, axis=0)
        intensity = (field_re * field_re + field_im * field_im) / float(W * W * BEAMS)
        return intensity.reshape(block_size, K // BIN, BIN, K // BIN, BIN).mean(axis=(2, 4))

    result = lax.map(probe_block, probes.reshape(PROBES // block_size, block_size, 2))
    return result.reshape(PROBES, K // BIN, K // BIN)
```

```python
import functools
import math

import jax
import jax.numpy as jnp
from jax import lax
from jax.experimental import pallas as pl
from jax.experimental.pallas import tpu as pltpu
from jax.sharding import PartitionSpec as P

IF = 4
BIN = 2
CAP = 2
PER_LIST = 2 * CAP
LANES = 128
GROUP = 16
ROWS = 16

two_pi = 2.0 * math.pi
f32 = jnp.float32
bf16 = jnp.bfloat16
i32 = jnp.int32


def iota(shape, dim):
    return lax.broadcasted_iota(i32, shape, dim)


def turns(index, window):
    return (two_pi / window) * jnp.bitwise_and(index, window - 1).astype(f32)


def bit_reversed(number, count):
    bits = count.bit_length() - 1
    return sum(((number >> b) & 1) << (bits - 1 - b) for b in range(bits))


def window_start(row, window, field_rows):
    start = jnp.right_shift(row, 2) - window // 2
    start = jnp.where(start < 0, start + field_rows, start)
    tile = jnp.right_shift(start, window.bit_length() - 1)
    return tile, jnp.bitwise_and(start, window - 1)


def times_i(pairs):
    return pltpu.roll(pairs, LANES // 2, pairs.ndim - 1)


def spectra_kernel(sizes, probes, smatrix, spectra, row_table, turn, column_table):
    window, kept, n_tile, n_beam = sizes
    share = kept // n_beam
    me_beam = lax.axis_index("beam")

    @pl.when(pl.program_id(0) == 0)
    def tables():
        shape = (2 * window, 2 * kept)
        x, part_in = iota(shape, 0) % window, iota(shape, 0) // window
        lane = iota(shape, 1)
        v, part_out = lane % kept - kept // 2, lane // kept
        angle = turns(x * v + (window // 4) * (part_out - part_in), window)
        column_table[...] = jnp.cos(angle).astype(bf16)

        shape = (2 * kept, 2 * window)
        line, turned = iota(shape, 0) % kept, iota(shape, 0) // kept
        r, part_in = iota(shape, 1) % window, iota(shape, 1) // window
        block = line // share
        owner = jnp.zeros_like(block)
        for pos in range(n_beam):
            owner = jnp.where(block == pos, jnp.bitwise_xor(me_beam, bit_reversed(pos, n_beam)), owner)
        u = owner * share + line % share - kept // 2
        angle = turns(u * r + (window // 4) * (turned - part_in), window)
        row_table[...] = jnp.cos(angle).astype(bf16)

        u = iota((share, LANES), 0) + me_beam * share - kept // 2
        lane = iota((share, LANES), 1)
        v = lane % kept - kept // 2
        for j in range(probes.shape[0]):
            _, offset = window_start(probes[j, 0], window, window * n_tile)
            shift = jnp.right_shift(probes[j, 1], 2) - window // 2
            angle = turns(u * offset + v * shift, window)
            turn[0, j] = jnp.cos(angle)
            turn[1, j] = jnp.where(lane < kept, -jnp.sin(angle), jnp.sin(angle))

    planes = smatrix.shape[1]
    flat = jnp.concatenate(
        [smatrix[0].reshape(planes * window, window), smatrix[1].reshape(planes * window, window)], axis=1
    )
    product = jnp.dot(flat, column_table[...], preferred_element_type=f32)
    spectra[...] = product.astype(bf16).reshape(spectra.shape)


def chosen(lists, me_tile, window, n_tile):
    before = jnp.where(me_tile == 0, n_tile - 1, me_tile - 1)
    rows, columns = [], []
    for probes in lists:
        picked = [[i32(0), i32(0)] for _ in range(PER_LIST)]
        seen = [i32(0), i32(0)]
        for j in range(probes.shape[0]):
            row, column = probes[j, 0], probes[j, 1]
            tile, _ = window_start(row, window, window * n_tile)
            for which, wanted in enumerate((me_tile, before)):
                match = tile == wanted
                for slot in range(CAP):
                    take = match & (seen[which] == slot)
                    held = picked[which * CAP + slot]
                    picked[which * CAP + slot] = [jnp.where(take, row, held[0]), jnp.where(take, column, held[1])]
                seen[which] = seen[which] + match.astype(i32)
        rows += [p[0] for p in picked]
        columns += [p[1] for p in picked]
    return rows, columns


def parts_kernel(sizes, *refs):
    window, kept, n_tile, n_beam = sizes
    lists = refs[:n_tile]
    beam_table, row_table, spectra, keep, send, coeff, waves = refs[n_tile:]
    share = kept // n_beam
    beams = spectra.shape[0]
    slots = n_tile * PER_LIST
    wide = beams * ROWS
    me_tile = lax.axis_index("tile")
    rows, columns = chosen(lists, me_tile, window, n_tile)
    offsets = [window_start(row, window, window * n_tile)[1] for row in rows]
    which = iota((slots, 1), 0)
    row_v = jnp.zeros((slots, 1), f32)
    column_v = jnp.zeros((slots, 1), f32)
    for s in range(slots):
        row_v = jnp.where(which == s, rows[s].astype(f32), row_v)
        column_v = jnp.where(which == s, columns[s].astype(f32), column_v)
    phase = beam_table[2:3, :] + two_pi / (window * IF) * (
        beam_table[0:1, :] * row_v + beam_table[1:2, :] * column_v
    )
    alpha = jnp.concatenate([jnp.cos(phase), -jnp.sin(phase)], axis=0).astype(bf16)
    spread = (iota((beams, wide), 1) // ROWS == iota((beams, wide), 0)).astype(f32).astype(bf16)
    alpha = jnp.dot(alpha, spread, preferred_element_type=f32)
    own_row = iota((ROWS, wide), 1) % ROWS == iota((ROWS, wide), 0)
    y_in = iota((ROWS, LANES), 0)
    lane = iota((kept, LANES), 1)
    sign = jnp.where(lane < kept, -1.0, 1.0)
    for first in range(0, slots, GROUP):
        for c in range(2):
            for p in range(GROUP):
                line = c * slots + first + p
                spot = (c * GROUP + p) * ROWS
                coeff[spot : spot + ROWS, :] = jnp.where(own_row, alpha[line : line + 1, :], 0.0).astype(bf16)
        for y in range(0, window, 2 * ROWS):
            pair = jnp.concatenate(
                [spectra[:, y + h : y + h + ROWS, :].reshape(wide, LANES) for h in (0, ROWS)], axis=1
            )
            made = jnp.dot(coeff[...], pair, preferred_element_type=f32)
            for h in range(2):
                y_here = y_in + (y + h * ROWS)
                for p in range(GROUP):
                    offset = offsets[first + p]
                    starts_here = p % PER_LIST < CAP
                    inside = y_here >= offset if starts_here else y_here < offset
                    for c in range(2):
                        spot = (c * GROUP + p) * ROWS
                        value = made[spot : spot + ROWS, h * LANES : (h + 1) * LANES]
                        waves[c, p, y + h * ROWS : y + (h + 1) * ROWS, :] = jnp.where(inside, value, 0.0).astype(bf16)
        for p in range(0, GROUP, PER_LIST):
            fields = []
            for q in range(p, p + PER_LIST, 2):
                pair = jnp.concatenate(
                    [waves[:, q + h].reshape(2 * window, LANES) for h in range(2)], axis=1
                )
                both = jnp.dot(row_table[...], pair, preferred_element_type=f32)
                for h in range(2):
                    value = both[:, h * LANES : (h + 1) * LANES]
                    fields.append(value[:kept] + times_i(value[kept:]) * sign)
            k = (first + p) // PER_LIST
            for pos in range(n_beam):
                block = jnp.concatenate([f[pos * share : (pos + 1) * share] for f in fields], axis=0).astype(bf16)
                half = n_beam // 2
                if pos < half:
                    keep[pos, k] = block
                else:
                    send[pos - half, k] = block


def result_kernel(sizes, all_beams, *refs):
    window, kept, n_tile, n_beam = sizes
    probes, turn = refs[:2]
    blocks = refs[2 : 2 + n_tile]
    out, staged, intensity = refs[2 + n_tile :]
    share = kept // n_beam
    count = probes.shape[0]
    me_tile = lax.axis_index("tile")
    for k in range(n_tile):
        block = blocks[k][...].astype(f32)
        for s in range(PER_LIST):
            staged[k * PER_LIST + s] = block[s * share : (s + 1) * share]
    tiles = [window_start(probes[j, 0], window, window * n_tile)[0] for j in range(count)]
    for j in range(count):
        slot = sum([(tiles[i] == tiles[j]).astype(i32) for i in range(j)], i32(0))
        following = jnp.where(tiles[j] == n_tile - 1, 0, tiles[j] + 1)
        field = (
            staged[jnp.bitwise_xor(tiles[j], me_tile) * PER_LIST + slot]
            + staged[jnp.bitwise_xor(following, me_tile) * PER_LIST + CAP + slot]
        )
        field = field * turn[0, j] + times_i(field) * turn[1, j]
        intensity[j * share : (j + 1) * share, :] = field * field
    height = count * share // BIN
    summed = intensity[pl.ds(0, height, stride=BIN), :]
    for b in range(1, BIN):
        summed = summed + intensity[pl.ds(b, height, stride=BIN), :]
    shape = (LANES, kept // BIN)
    bins = (iota(shape, 0) % kept // BIN == iota(shape, 1)).astype(f32)
    binned = jnp.dot(summed, bins, precision=lax.Precision.HIGHEST, preferred_element_type=f32)
    binned = binned * (1.0 / (BIN * BIN * window * window * all_beams))
    for j in range(count):
        out[j] = binned[j * (share // BIN) : (j + 1) * (share // BIN)]


VMEM = pl.BlockSpec(memory_space=pltpu.VMEM)
SMEM = pl.BlockSpec(memory_space=pltpu.SMEM)


def params(**more):
    return pltpu.CompilerParams(vmem_limit_bytes=48 * 1024 * 1024, **more)


def swapped(array, axis, by):
    return lax.ppermute(array, axis, [(i, i ^ by) for i in range(lax.axis_size(axis))])


def per_device(smatrix, beam_table, probes):
    _, beams, window, _ = smatrix.shape
    kept = window // 2
    n_tile = lax.axis_size("tile")
    n_beam = lax.axis_size("beam")
    sizes = (window, kept, n_tile, n_beam)
    share = kept // n_beam
    slots = n_tile * PER_LIST
    count = probes.shape[0]

    lists = [probes] + [swapped(probes, "tile", k) for k in range(1, n_tile)]

    step = 8
    spectra, row_table, turn = pl.pallas_call(
        functools.partial(spectra_kernel, sizes),
        grid=(beams // step,),
        in_specs=[SMEM, pl.BlockSpec((2, step, window, window), lambda i: (0, i, 0, 0))],
        out_specs=[
            pl.BlockSpec((step, window, 2 * kept), lambda i: (i, 0, 0)),
            pl.BlockSpec((2 * kept, 2 * window), lambda i: (0, 0)),
            pl.BlockSpec((2, count, share, LANES), lambda i: (0, 0, 0, 0)),
        ],
        out_shape=[
            jax.ShapeDtypeStruct((beams, window, 2 * kept), bf16),
            jax.ShapeDtypeStruct((2 * kept, 2 * window), bf16),
            jax.ShapeDtypeStruct((2, count, share, LANES), f32),
        ],
        scratch_shapes=[pltpu.VMEM((2 * window, 2 * kept), bf16)],
        compiler_params=params(),
        cost_estimate=pl.CostEstimate(
            flops=2 * beams * window * 4 * window * kept, bytes_accessed=smatrix.size * 3, transcendentals=0
        ),
        name="spectra",
    )(probes, smatrix)

    half = jax.ShapeDtypeStruct((n_beam // 2, n_tile, PER_LIST * share, LANES), bf16)
    keep, send = pl.pallas_call(
        functools.partial(parts_kernel, sizes),
        in_specs=[SMEM] * n_tile + [VMEM] * 3,
        out_specs=[VMEM] * 2,
        out_shape=[half, half],
        scratch_shapes=[
            pltpu.VMEM((2 * GROUP * ROWS, beams * ROWS), bf16),
            pltpu.VMEM((2, GROUP, window, LANES), bf16),
        ],
        compiler_params=params(),
        cost_estimate=pl.CostEstimate(
            flops=2 * slots * 2 * ROWS * beams * window * LANES, bytes_accessed=4 * 1024 * 1024, transcendentals=0
        ),
        name="parts",
    )(*lists, beam_table, row_table, spectra)

    by = 1
    while by < n_beam:
        arrived = swapped(send, "beam", by)
        total = (keep.astype(f32) + arrived.astype(f32)).astype(bf16)
        by *= 2
        middle = total.shape[0] // 2
        keep, send = total[:middle], total[middle:]
    mine = total[0]
    blocks = [mine[0]] + [swapped(mine[k], "tile", k) for k in range(1, n_tile)]

    return pl.pallas_call(
        functools.partial(result_kernel, sizes, beams * n_beam),
        in_specs=[SMEM] + [VMEM] * (1 + n_tile),
        out_specs=VMEM,
        out_shape=jax.ShapeDtypeStruct((count, share // BIN, kept // BIN), f32),
        scratch_shapes=[pltpu.VMEM((slots, share, LANES), f32), pltpu.VMEM((count * share, LANES), f32)],
        compiler_params=params(),
        name="result",
    )(probes, turn, *blocks)


def solution(mesh):
    in_specs = (
        P(None, ("groups", "beam"), "tile", None),
        P(None, "beam"),
        P(("groups", "tile"), None),
    )
    out_specs = P(("groups", "tile"), "beam", None)
    return jax.shard_map(
        per_device, mesh=mesh, in_specs=in_specs, out_specs=out_specs, check_vma=False
    )
```

```python
import functools
import math

import jax
import jax.numpy as jnp
from jax import lax
from jax.experimental import pallas as pl
from jax.experimental.pallas import tpu as pltpu
from jax.sharding import PartitionSpec as P

IF = 4
BIN = 2
CAP = 2
PER_LIST = 2 * CAP
LANES = 128
GROUP = 16
CHUNKS = 1
ROWS = 16

two_pi = 2.0 * math.pi
f32 = jnp.float32
bf16 = jnp.bfloat16
i32 = jnp.int32


def iota(shape, dim):
    return lax.broadcasted_iota(i32, shape, dim)


def turns(index, window):
    return (two_pi / window) * jnp.bitwise_and(index, window - 1).astype(f32)


def bit_reversed(number, count):
    bits = count.bit_length() - 1
    return sum(((number >> b) & 1) << (bits - 1 - b) for b in range(bits))


def window_start(row, window, field_rows):
    start = jnp.right_shift(row, 2) - window // 2
    start = jnp.where(start < 0, start + field_rows, start)
    tile = jnp.right_shift(start, window.bit_length() - 1)
    return tile, jnp.bitwise_and(start, window - 1)


def times_i(pairs):
    return pltpu.roll(pairs, LANES // 2, pairs.ndim - 1)


def spectra_kernel(sizes, probes_hbm, smatrix_hbm, spectra, row_table, turn, column_table, smatrix, probes, sems):
    window, kept, n_tile, n_beam = sizes
    share = kept // n_beam
    me_beam = lax.axis_index("beam")
    planes = smatrix.shape[1] // CHUNKS
    chunks = [pl.ds(i * planes, planes) for i in range(CHUNKS)]
    copies = [
        pltpu.make_async_copy(smatrix_hbm.at[:, chunk], smatrix.at[:, chunk], sems.at[i])
        for i, chunk in enumerate(chunks)
    ]
    for copy in copies:
        copy.start()
    listed = pltpu.make_async_copy(probes_hbm, probes, sems.at[CHUNKS])
    listed.start()

    shape = (2 * window, 2 * kept)
    x, part_in = iota(shape, 0) % window, iota(shape, 0) // window
    lane = iota(shape, 1)
    v, part_out = lane % kept - kept // 2, lane // kept
    angle = turns(x * v + (window // 4) * (part_out - part_in), window)
    column_table[...] = jnp.cos(angle).astype(bf16)

    shape = (2 * kept, 2 * window)
    line, turned = iota(shape, 0) % kept, iota(shape, 0) // kept
    r, part_in = iota(shape, 1) % window, iota(shape, 1) // window
    block = line // share
    owner = jnp.zeros_like(block)
    for pos in range(n_beam):
        owner = jnp.where(block == pos, jnp.bitwise_xor(me_beam, bit_reversed(pos, n_beam)), owner)
    u = owner * share + line % share - kept // 2
    angle = turns(u * r + (window // 4) * (turned - part_in), window)
    row_table[...] = jnp.cos(angle).astype(bf16)

    u = iota((share, LANES), 0) + me_beam * share - kept // 2
    lane = iota((share, LANES), 1)
    v = lane % kept - kept // 2
    listed.wait()
    for j in range(probes.shape[1]):
        _, offset = window_start(probes[0, j], window, window * n_tile)
        shift = jnp.right_shift(probes[1, j], 2) - window // 2
        angle = turns(u * offset + v * shift, window)
        turn[0, j] = jnp.cos(angle)
        turn[1, j] = jnp.where(lane < kept, -jnp.sin(angle), jnp.sin(angle))

    for copy, chunk in zip(copies, chunks):
        copy.wait()
        flat = jnp.concatenate([smatrix[c, chunk].reshape(planes * window, window) for c in range(2)], axis=1)
        product = jnp.dot(flat, column_table[...], preferred_element_type=f32)
        spectra[chunk] = product.astype(bf16).reshape(planes, window, 2 * kept)


def chosen(lists, me_tile, window, n_tile):
    before = jnp.where(me_tile == 0, n_tile - 1, me_tile - 1)
    rows, columns = [], []
    for probes in lists:
        picked = [[i32(0), i32(0)] for _ in range(PER_LIST)]
        seen = [i32(0), i32(0)]
        for j in range(probes.shape[1]):
            row, column = probes[0, j], probes[1, j]
            tile, _ = window_start(row, window, window * n_tile)
            for which, wanted in enumerate((me_tile, before)):
                match = tile == wanted
                for slot in range(CAP):
                    take = match & (seen[which] == slot)
                    held = picked[which * CAP + slot]
                    picked[which * CAP + slot] = [jnp.where(take, row, held[0]), jnp.where(take, column, held[1])]
                seen[which] = seen[which] + match.astype(i32)
        rows += [p[0] for p in picked]
        columns += [p[1] for p in picked]
    return rows, columns


def parts_kernel(sizes, *refs):
    window, kept, n_tile, n_beam = sizes
    lists = refs[:n_tile]
    beam_table, row_table, spectra, keep, send, coeff, waves = refs[n_tile:]
    share = kept // n_beam
    beams = spectra.shape[0]
    slots = n_tile * PER_LIST
    wide = beams * ROWS
    me_tile = lax.axis_index("tile")
    rows, columns = chosen(lists, me_tile, window, n_tile)
    offsets = [window_start(row, window, window * n_tile)[1] for row in rows]
    which = iota((slots, 1), 0)
    row_v = jnp.zeros((slots, 1), f32)
    column_v = jnp.zeros((slots, 1), f32)
    for s in range(slots):
        row_v = jnp.where(which == s, rows[s].astype(f32), row_v)
        column_v = jnp.where(which == s, columns[s].astype(f32), column_v)
    phase = beam_table[2:3, :] + two_pi / (window * IF) * (
        beam_table[0:1, :] * row_v + beam_table[1:2, :] * column_v
    )
    alpha = jnp.concatenate([jnp.cos(phase), -jnp.sin(phase)], axis=0).astype(bf16)
    spread = (iota((beams, wide), 1) // ROWS == iota((beams, wide), 0)).astype(f32).astype(bf16)
    alpha = jnp.dot(alpha, spread, preferred_element_type=f32)
    own_row = iota((ROWS, wide), 1) % ROWS == iota((ROWS, wide), 0)
    y_in = iota((ROWS, LANES), 0)
    lane = iota((kept, LANES), 1)
    sign = jnp.where(lane < kept, -1.0, 1.0)
    for first in range(0, slots, GROUP):
        for c in range(2):
            for p in range(GROUP):
                line = c * slots + first + p
                spot = (c * GROUP + p) * ROWS
                coeff[spot : spot + ROWS, :] = jnp.where(own_row, alpha[line : line + 1, :], 0.0).astype(bf16)
        for y in range(0, window, 2 * ROWS):
            pair = jnp.concatenate(
                [spectra[:, y + h : y + h + ROWS, :].reshape(wide, LANES) for h in (0, ROWS)], axis=1
            )
            made = jnp.dot(coeff[...], pair, preferred_element_type=f32)
            for h in range(2):
                y_here = y_in + (y + h * ROWS)
                for p in range(GROUP):
                    offset = offsets[first + p]
                    starts_here = p % PER_LIST < CAP
                    inside = y_here >= offset if starts_here else y_here < offset
                    for c in range(2):
                        spot = (c * GROUP + p) * ROWS
                        value = made[spot : spot + ROWS, h * LANES : (h + 1) * LANES]
                        waves[c, p, y + h * ROWS : y + (h + 1) * ROWS, :] = jnp.where(inside, value, 0.0).astype(bf16)
        for p in range(0, GROUP, PER_LIST):
            fields = []
            for q in range(p, p + PER_LIST, 2):
                pair = jnp.concatenate(
                    [waves[:, q + h].reshape(2 * window, LANES) for h in range(2)], axis=1
                )
                both = jnp.dot(row_table[...], pair, preferred_element_type=f32)
                for h in range(2):
                    value = both[:, h * LANES : (h + 1) * LANES]
                    fields.append(value[:kept] + times_i(value[kept:]) * sign)
            k = (first + p) // PER_LIST
            for pos in range(n_beam):
                block = jnp.concatenate([f[pos * share : (pos + 1) * share] for f in fields], axis=0).astype(bf16)
                half = n_beam // 2
                if pos < half:
                    keep[pos, k] = block
                else:
                    send[pos - half, k] = block


def result_kernel(sizes, all_beams, *refs):
    window, kept, n_tile, n_beam = sizes
    probes, turn = refs[:2]
    blocks = refs[2 : 2 + n_tile]
    out, staged, intensity = refs[2 + n_tile :]
    share = kept // n_beam
    count = probes.shape[1]
    me_tile = lax.axis_index("tile")
    for k in range(n_tile):
        block = blocks[k][...].astype(f32)
        for s in range(PER_LIST):
            staged[k * PER_LIST + s] = block[s * share : (s + 1) * share]
    tiles = [window_start(probes[0, j], window, window * n_tile)[0] for j in range(count)]
    for j in range(count):
        slot = sum([(tiles[i] == tiles[j]).astype(i32) for i in range(j)], i32(0))
        following = jnp.where(tiles[j] == n_tile - 1, 0, tiles[j] + 1)
        field = (
            staged[jnp.bitwise_xor(tiles[j], me_tile) * PER_LIST + slot]
            + staged[jnp.bitwise_xor(following, me_tile) * PER_LIST + CAP + slot]
        )
        field = field * turn[0, j] + times_i(field) * turn[1, j]
        intensity[j * share : (j + 1) * share, :] = field * field
    height = count * share // BIN
    summed = intensity[pl.ds(0, height, stride=BIN), :]
    for b in range(1, BIN):
        summed = summed + intensity[pl.ds(b, height, stride=BIN), :]
    shape = (LANES, kept // BIN)
    bins = (iota(shape, 0) % kept // BIN == iota(shape, 1)).astype(f32)
    binned = jnp.dot(summed, bins, precision=lax.Precision.HIGHEST, preferred_element_type=f32)
    binned = binned * (1.0 / (BIN * BIN * window * window * all_beams))
    for j in range(count):
        out[j] = binned[j * (share // BIN) : (j + 1) * (share // BIN)]


VMEM = pl.BlockSpec(memory_space=pltpu.VMEM)
HBM = pl.BlockSpec(memory_space=pltpu.HBM)
SMEM = pl.BlockSpec(memory_space=pltpu.SMEM)


def params(mib=16):
    return pltpu.CompilerParams(vmem_limit_bytes=mib * 1024 * 1024)


def swapped(array, axis, by):
    return lax.ppermute(array, axis, [(i, i ^ by) for i in range(lax.axis_size(axis))])


def per_device(smatrix, beam_table, probes):
    _, beams, window, _ = smatrix.shape
    kept = window // 2
    n_tile = lax.axis_size("tile")
    n_beam = lax.axis_size("beam")
    sizes = (window, kept, n_tile, n_beam)
    share = kept // n_beam
    slots = n_tile * PER_LIST
    count = probes.shape[0]

    probes = probes.T
    lists = [probes] + [swapped(probes, "tile", k) for k in range(1, n_tile)]

    spectra, row_table, turn = pl.pallas_call(
        functools.partial(spectra_kernel, sizes),
        in_specs=[HBM, HBM],
        out_specs=[VMEM] * 3,
        out_shape=[
            jax.ShapeDtypeStruct((beams, window, 2 * kept), bf16),
            jax.ShapeDtypeStruct((2 * kept, 2 * window), bf16),
            jax.ShapeDtypeStruct((2, count, share, LANES), f32),
        ],
        scratch_shapes=[
            pltpu.VMEM((2 * window, 2 * kept), bf16),
            pltpu.VMEM(smatrix.shape, bf16),
            pltpu.SMEM(probes.shape, i32),
            pltpu.SemaphoreType.DMA((CHUNKS + 1,)),
        ],
        compiler_params=params(48),
        cost_estimate=pl.CostEstimate(
            flops=2 * beams * window * 4 * window * kept, bytes_accessed=smatrix.size * 3, transcendentals=0
        ),
        name="spectra",
    )(pltpu.with_memory_space_constraint(probes, pltpu.HBM), pltpu.with_memory_space_constraint(smatrix, pltpu.HBM))

    half = jax.ShapeDtypeStruct((n_beam // 2, n_tile, PER_LIST * share, LANES), bf16)
    keep, send = pl.pallas_call(
        functools.partial(parts_kernel, sizes),
        in_specs=[SMEM] * n_tile + [VMEM] * 3,
        out_specs=[VMEM] * 2,
        out_shape=[half, half],
        scratch_shapes=[
            pltpu.VMEM((2 * GROUP * ROWS, beams * ROWS), bf16),
            pltpu.VMEM((2, GROUP, window, LANES), bf16),
        ],
        compiler_params=params(),
        cost_estimate=pl.CostEstimate(
            flops=2 * slots * 2 * ROWS * beams * window * LANES, bytes_accessed=4 * 1024 * 1024, transcendentals=0
        ),
        name="parts",
    )(*lists, beam_table, row_table, spectra)

    by = 1
    while by < n_beam:
        arrived = swapped(send, "beam", by)
        total = (keep.astype(f32) + arrived.astype(f32)).astype(bf16)
        by *= 2
        middle = total.shape[0] // 2
        keep, send = total[:middle], total[middle:]
    mine = total[0]
    blocks = [mine[0]] + [swapped(mine[k], "tile", k) for k in range(1, n_tile)]

    return pl.pallas_call(
        functools.partial(result_kernel, sizes, beams * n_beam),
        in_specs=[SMEM] + [VMEM] * (1 + n_tile),
        out_specs=VMEM,
        out_shape=jax.ShapeDtypeStruct((count, share // BIN, kept // BIN), f32),
        scratch_shapes=[pltpu.VMEM((slots, share, LANES), f32), pltpu.VMEM((count * share, LANES), f32)],
        compiler_params=params(),
        name="result",
    )(probes, turn, *blocks)


def solution(mesh):
    in_specs = (
        P(None, ("groups", "beam"), "tile", None),
        P(None, "beam"),
        P(("groups", "tile"), None),
    )
    out_specs = P(("groups", "tile"), "beam", None)
    return jax.shard_map(
        per_device, mesh=mesh, in_specs=in_specs, out_specs=out_specs, check_vma=False
    )
```

```python
import functools
import math

import jax
import jax.numpy as jnp
from jax import lax
from jax.experimental import pallas as pl
from jax.experimental.pallas import tpu as pltpu
from jax.sharding import PartitionSpec as P

IF = 4
BIN = 2
CAP = 2
PER_LIST = 2 * CAP
LANES = 128
GROUP = 16
CHUNKS = 1
ROWS = 16

LISTS_ORDER = (0, 2, 3, 1)
RESULTS_ORDER = (0, 1, 2, 3)


def orders(n_tile):
    if n_tile == 4:
        return LISTS_ORDER, RESULTS_ORDER
    return tuple(range(n_tile)), tuple(range(n_tile))


two_pi = 2.0 * math.pi
f32 = jnp.float32
bf16 = jnp.bfloat16
i32 = jnp.int32


def iota(shape, dim):
    return lax.broadcasted_iota(i32, shape, dim)


def turns(index, window):
    return (two_pi / window) * jnp.bitwise_and(index, window - 1).astype(f32)


def bit_reversed(number, count):
    bits = count.bit_length() - 1
    return sum(((number >> b) & 1) << (bits - 1 - b) for b in range(bits))


def window_start(row, window, field_rows):
    start = jnp.right_shift(row, 2) - window // 2
    start = jnp.where(start < 0, start + field_rows, start)
    tile = jnp.right_shift(start, window.bit_length() - 1)
    return tile, jnp.bitwise_and(start, window - 1)


def times_i(pairs):
    return pltpu.roll(pairs, LANES // 2, pairs.ndim - 1)


def spectra_kernel(sizes, probes_hbm, smatrix_hbm, spectra, row_table, turn, column_table, smatrix, probes, sems):
    window, kept, n_tile, n_beam = sizes
    share = kept // n_beam
    me_beam = lax.axis_index("beam")
    planes = smatrix.shape[1] // CHUNKS
    chunks = [pl.ds(i * planes, planes) for i in range(CHUNKS)]
    copies = [
        pltpu.make_async_copy(smatrix_hbm.at[:, chunk], smatrix.at[:, chunk], sems.at[i])
        for i, chunk in enumerate(chunks)
    ]
    for copy in copies:
        copy.start()
    listed = pltpu.make_async_copy(probes_hbm, probes, sems.at[CHUNKS])
    listed.start()

    shape = (2 * window, 2 * kept)
    x, part_in = iota(shape, 0) % window, iota(shape, 0) // window
    lane = iota(shape, 1)
    v, part_out = lane % kept - kept // 2, lane // kept
    angle = turns(x * v + (window // 4) * (part_out - part_in), window)
    column_table[...] = jnp.cos(angle).astype(bf16)

    shape = (2 * kept, 2 * window)
    line, turned = iota(shape, 0) % kept, iota(shape, 0) // kept
    r, part_in = iota(shape, 1) % window, iota(shape, 1) // window
    block = line // share
    owner = jnp.zeros_like(block)
    for pos in range(n_beam):
        owner = jnp.where(block == pos, jnp.bitwise_xor(me_beam, bit_reversed(pos, n_beam)), owner)
    u = owner * share + line % share - kept // 2
    angle = turns(u * r + (window // 4) * (turned - part_in), window)
    row_table[...] = jnp.cos(angle).astype(bf16)

    u = iota((share, LANES), 0) + me_beam * share - kept // 2
    lane = iota((share, LANES), 1)
    v = lane % kept - kept // 2
    listed.wait()
    for j in range(probes.shape[1]):
        _, offset = window_start(probes[0, j], window, window * n_tile)
        shift = jnp.right_shift(probes[1, j], 2) - window // 2
        angle = turns(u * offset + v * shift, window)
        turn[0, j] = jnp.cos(angle)
        turn[1, j] = jnp.where(lane < kept, -jnp.sin(angle), jnp.sin(angle))

    for copy, chunk in zip(copies, chunks):
        copy.wait()
        flat = jnp.concatenate([smatrix[c, chunk].reshape(planes * window, window) for c in range(2)], axis=1)
        product = jnp.dot(flat, column_table[...], preferred_element_type=f32)
        spectra[chunk] = product.astype(bf16).reshape(planes, window, 2 * kept)


def chosen(lists, me_tile, window, n_tile):
    before = jnp.where(me_tile == 0, n_tile - 1, me_tile - 1)
    rows, columns = [], []
    for probes in lists:
        picked = [[i32(0), i32(0)] for _ in range(PER_LIST)]
        seen = [i32(0), i32(0)]
        for j in range(probes.shape[1]):
            row, column = probes[0, j], probes[1, j]
            tile, _ = window_start(row, window, window * n_tile)
            for which, wanted in enumerate((me_tile, before)):
                match = tile == wanted
                for slot in range(CAP):
                    take = match & (seen[which] == slot)
                    held = picked[which * CAP + slot]
                    picked[which * CAP + slot] = [jnp.where(take, row, held[0]), jnp.where(take, column, held[1])]
                seen[which] = seen[which] + match.astype(i32)
        rows += [p[0] for p in picked]
        columns += [p[1] for p in picked]
    return rows, columns


def parts_kernel(sizes, *refs):
    window, kept, n_tile, n_beam = sizes
    lists = in_order(refs[:n_tile], orders(n_tile)[0])
    beam_table, row_table, spectra, keep, send, coeff, waves = refs[n_tile:]
    share = kept // n_beam
    beams = spectra.shape[0]
    slots = n_tile * PER_LIST
    wide = beams * ROWS
    me_tile = lax.axis_index("tile")
    rows, columns = chosen(lists, me_tile, window, n_tile)
    offsets = [window_start(row, window, window * n_tile)[1] for row in rows]
    which = iota((slots, 1), 0)
    row_v = jnp.zeros((slots, 1), f32)
    column_v = jnp.zeros((slots, 1), f32)
    for s in range(slots):
        row_v = jnp.where(which == s, rows[s].astype(f32), row_v)
        column_v = jnp.where(which == s, columns[s].astype(f32), column_v)
    phase = beam_table[2:3, :] + two_pi / (window * IF) * (
        beam_table[0:1, :] * row_v + beam_table[1:2, :] * column_v
    )
    alpha = jnp.concatenate([jnp.cos(phase), -jnp.sin(phase)], axis=0).astype(bf16)
    spread = (iota((beams, wide), 1) // ROWS == iota((beams, wide), 0)).astype(f32).astype(bf16)
    alpha = jnp.dot(alpha, spread, preferred_element_type=f32)
    own_row = iota((ROWS, wide), 1) % ROWS == iota((ROWS, wide), 0)
    y_in = iota((ROWS, LANES), 0)
    lane = iota((kept, LANES), 1)
    sign = jnp.where(lane < kept, -1.0, 1.0)
    for first in range(0, slots, GROUP):
        for c in range(2):
            for p in range(GROUP):
                line = c * slots + first + p
                spot = (c * GROUP + p) * ROWS
                coeff[spot : spot + ROWS, :] = jnp.where(own_row, alpha[line : line + 1, :], 0.0).astype(bf16)
        for y in range(0, window, 2 * ROWS):
            pair = jnp.concatenate(
                [spectra[:, y + h : y + h + ROWS, :].reshape(wide, LANES) for h in (0, ROWS)], axis=1
            )
            made = jnp.dot(coeff[...], pair, preferred_element_type=f32)
            for h in range(2):
                y_here = y_in + (y + h * ROWS)
                for p in range(GROUP):
                    offset = offsets[first + p]
                    starts_here = p % PER_LIST < CAP
                    inside = y_here >= offset if starts_here else y_here < offset
                    for c in range(2):
                        spot = (c * GROUP + p) * ROWS
                        value = made[spot : spot + ROWS, h * LANES : (h + 1) * LANES]
                        waves[c, p, y + h * ROWS : y + (h + 1) * ROWS, :] = jnp.where(inside, value, 0.0).astype(bf16)
        for p in range(0, GROUP, PER_LIST):
            fields = []
            for q in range(p, p + PER_LIST, 2):
                pair = jnp.concatenate(
                    [waves[:, q + h].reshape(2 * window, LANES) for h in range(2)], axis=1
                )
                both = jnp.dot(row_table[...], pair, preferred_element_type=f32)
                for h in range(2):
                    value = both[:, h * LANES : (h + 1) * LANES]
                    fields.append(value[:kept] + times_i(value[kept:]) * sign)
            k = (first + p) // PER_LIST
            for pos in range(n_beam):
                block = jnp.concatenate([f[pos * share : (pos + 1) * share] for f in fields], axis=0).astype(bf16)
                half = n_beam // 2
                if pos < half:
                    keep[pos, k] = block
                else:
                    send[pos - half, k] = block


def result_kernel(sizes, all_beams, *refs):
    window, kept, n_tile, n_beam = sizes
    probes, turn = refs[:2]
    blocks = in_order(refs[2 : 2 + n_tile], orders(n_tile)[1])
    out, staged, intensity = refs[2 + n_tile :]
    share = kept // n_beam
    count = probes.shape[1]
    me_tile = lax.axis_index("tile")
    for k in range(n_tile):
        block = blocks[k][...].astype(f32)
        for s in range(PER_LIST):
            staged[k * PER_LIST + s] = block[s * share : (s + 1) * share]
    def place(tile):
        return jnp.where(tile < me_tile, tile + n_tile, tile) - me_tile

    tiles = [window_start(probes[0, j], window, window * n_tile)[0] for j in range(count)]
    for j in range(count):
        slot = sum([(tiles[i] == tiles[j]).astype(i32) for i in range(j)], i32(0))
        following = jnp.where(tiles[j] == n_tile - 1, 0, tiles[j] + 1)
        field = (
            staged[place(tiles[j]) * PER_LIST + slot]
            + staged[place(following) * PER_LIST + CAP + slot]
        )
        field = field * turn[0, j] + times_i(field) * turn[1, j]
        intensity[j * share : (j + 1) * share, :] = field * field
    height = count * share // BIN
    summed = intensity[pl.ds(0, height, stride=BIN), :]
    for b in range(1, BIN):
        summed = summed + intensity[pl.ds(b, height, stride=BIN), :]
    shape = (LANES, kept // BIN)
    bins = (iota(shape, 0) % kept // BIN == iota(shape, 1)).astype(f32)
    binned = jnp.dot(summed, bins, precision=lax.Precision.HIGHEST, preferred_element_type=f32)
    binned = binned * (1.0 / (BIN * BIN * window * window * all_beams))
    for j in range(count):
        out[j] = binned[j * (share // BIN) : (j + 1) * (share // BIN)]


VMEM = pl.BlockSpec(memory_space=pltpu.VMEM)
HBM = pl.BlockSpec(memory_space=pltpu.HBM)
SMEM = pl.BlockSpec(memory_space=pltpu.SMEM)


def params(mib=16):
    return pltpu.CompilerParams(vmem_limit_bytes=mib * 1024 * 1024)


def swapped(array, axis, by):
    return lax.ppermute(array, axis, [(i, i ^ by) for i in range(lax.axis_size(axis))])


def shifted(arrays, way, order):
    size = lax.axis_size("tile")
    return [
        lax.ppermute(arrays[k], "tile", [(i, (i + way * k) % size) for i in range(size)]) if k else arrays[0]
        for k in order
    ]


def in_order(refs, order):
    return [refs[order.index(k)] for k in range(len(order))]


def per_device(smatrix, beam_table, probes):
    _, beams, window, _ = smatrix.shape
    kept = window // 2
    n_tile = lax.axis_size("tile")
    n_beam = lax.axis_size("beam")
    sizes = (window, kept, n_tile, n_beam)
    share = kept // n_beam
    slots = n_tile * PER_LIST
    count = probes.shape[0]

    probes = probes.T
    lists_order, results_order = orders(n_tile)
    lists = shifted([probes] * n_tile, 1, lists_order)

    spectra, row_table, turn = pl.pallas_call(
        functools.partial(spectra_kernel, sizes),
        in_specs=[HBM, HBM],
        out_specs=[VMEM] * 3,
        out_shape=[
            jax.ShapeDtypeStruct((beams, window, 2 * kept), bf16),
            jax.ShapeDtypeStruct((2 * kept, 2 * window), bf16),
            jax.ShapeDtypeStruct((2, count, share, LANES), f32),
        ],
        scratch_shapes=[
            pltpu.VMEM((2 * window, 2 * kept), bf16),
            pltpu.VMEM(smatrix.shape, bf16),
            pltpu.SMEM(probes.shape, i32),
            pltpu.SemaphoreType.DMA((CHUNKS + 1,)),
        ],
        compiler_params=params(48),
        cost_estimate=pl.CostEstimate(
            flops=2 * beams * window * 4 * window * kept, bytes_accessed=smatrix.size * 3, transcendentals=0
        ),
        name="spectra",
    )(pltpu.with_memory_space_constraint(probes, pltpu.HBM), pltpu.with_memory_space_constraint(smatrix, pltpu.HBM))

    half = jax.ShapeDtypeStruct((n_beam // 2, n_tile, PER_LIST * share, LANES), bf16)
    keep, send = pl.pallas_call(
        functools.partial(parts_kernel, sizes),
        in_specs=[SMEM] * n_tile + [VMEM] * 3,
        out_specs=[VMEM] * 2,
        out_shape=[half, half],
        scratch_shapes=[
            pltpu.VMEM((2 * GROUP * ROWS, beams * ROWS), bf16),
            pltpu.VMEM((2, GROUP, window, LANES), bf16),
        ],
        compiler_params=params(),
        cost_estimate=pl.CostEstimate(
            flops=2 * slots * 2 * ROWS * beams * window * LANES, bytes_accessed=4 * 1024 * 1024, transcendentals=0
        ),
        name="parts",
    )(*lists, beam_table, row_table, spectra)

    by = 1
    while by < n_beam:
        arrived = swapped(send, "beam", by)
        total = (keep.astype(f32) + arrived.astype(f32)).astype(bf16)
        by *= 2
        middle = total.shape[0] // 2
        keep, send = total[:middle], total[middle:]
    mine = total[0]
    blocks = shifted(mine, -1, results_order)

    return pl.pallas_call(
        functools.partial(result_kernel, sizes, beams * n_beam),
        in_specs=[SMEM] + [VMEM] * (1 + n_tile),
        out_specs=VMEM,
        out_shape=jax.ShapeDtypeStruct((count, share // BIN, kept // BIN), f32),
        scratch_shapes=[pltpu.VMEM((slots, share, LANES), f32), pltpu.VMEM((count * share, LANES), f32)],
        compiler_params=params(),
        name="result",
    )(probes, turn, *blocks)


def solution(mesh):
    in_specs = (
        P(None, ("groups", "beam"), "tile", None),
        P(None, "beam"),
        P(("groups", "tile"), None),
    )
    out_specs = P(("groups", "tile"), "beam", None)
    return jax.shard_map(
        per_device, mesh=mesh, in_specs=in_specs, out_specs=out_specs, check_vma=False
    )
```

```python
import functools
import math

import jax
import jax.numpy as jnp
from jax import lax
from jax.experimental import pallas as pl
from jax.experimental.pallas import tpu as pltpu
from jax.sharding import PartitionSpec as P

IF = 4
BIN = 2
CAP = 2
PER_LIST = 2 * CAP
LANES = 128
GROUP = 16
CHUNKS = 1
ROWS = 16

LISTS_ORDER = (0, 2, 3, 1)
RESULTS_ORDER = (0, 1, 2, 3)


def orders(n_tile):
    if n_tile == 4:
        return LISTS_ORDER, RESULTS_ORDER
    return tuple(range(n_tile)), tuple(range(n_tile))


two_pi = 2.0 * math.pi
f32 = jnp.float32
bf16 = jnp.bfloat16
i32 = jnp.int32


def iota(shape, dim):
    return lax.broadcasted_iota(i32, shape, dim)


def turns(index, window):
    return (two_pi / window) * jnp.bitwise_and(index, window - 1).astype(f32)


def bit_reversed(number, count):
    bits = count.bit_length() - 1
    return sum(((number >> b) & 1) << (bits - 1 - b) for b in range(bits))


def window_start(row, window, field_rows):
    start = jnp.right_shift(row, 2) - window // 2
    start = jnp.where(start < 0, start + field_rows, start)
    tile = jnp.right_shift(start, window.bit_length() - 1)
    return tile, jnp.bitwise_and(start, window - 1)


def times_i(pairs):
    return pltpu.roll(pairs, LANES // 2, pairs.ndim - 1)


def spectra_kernel(sizes, probes_hbm, smatrix_hbm, spectra, row_table, turn, select, column_table, smatrix, probes, sems):
    window, kept, n_tile, n_beam = sizes
    share = kept // n_beam
    me_beam = lax.axis_index("beam")
    me_tile = lax.axis_index("tile")
    planes = smatrix.shape[1] // CHUNKS
    chunks = [pl.ds(i * planes, planes) for i in range(CHUNKS)]
    copies = [
        pltpu.make_async_copy(smatrix_hbm.at[:, chunk], smatrix.at[:, chunk], sems.at[i])
        for i, chunk in enumerate(chunks)
    ]
    for copy in copies:
        copy.start()
    listed = pltpu.make_async_copy(probes_hbm, probes, sems.at[CHUNKS])
    listed.start()

    shape = (2 * window, 2 * kept)
    x, part_in = iota(shape, 0) % window, iota(shape, 0) // window
    lane = iota(shape, 1)
    v, part_out = lane % kept - kept // 2, lane // kept
    angle = turns(x * v + (window // 4) * (part_out - part_in), window)
    column_table[...] = jnp.cos(angle).astype(bf16)

    shape = (2 * kept, 2 * window)
    line, turned = iota(shape, 0) % kept, iota(shape, 0) // kept
    r, part_in = iota(shape, 1) % window, iota(shape, 1) // window
    block = line // share
    owner = jnp.zeros_like(block)
    for pos in range(n_beam):
        owner = jnp.where(block == pos, jnp.bitwise_xor(me_beam, bit_reversed(pos, n_beam)), owner)
    u = owner * share + line % share - kept // 2
    angle = turns(u * r + (window // 4) * (turned - part_in), window)
    row_table[...] = jnp.cos(angle).astype(bf16)

    u = iota((share, LANES), 0) + me_beam * share - kept // 2
    lane = iota((share, LANES), 1)
    v = lane % kept - kept // 2
    listed.wait()
    shape = (select.shape[0], select.shape[1])
    window_of, slot_of = iota(shape, 0) // share, iota(shape, 1) // share
    wanted = (slot_of == -1, slot_of == -1)
    tiles = []
    for j in range(probes.shape[1]):
        tile, offset = window_start(probes[0, j], window, window * n_tile)
        following = jnp.where(tile == n_tile - 1, 0, tile + 1)
        rank = sum([(t == tile).astype(i32) for t in tiles], i32(0))
        tiles.append(tile)
        spots = [
            (jnp.where(t < me_tile, t + n_tile, t) - me_tile) * PER_LIST + base + rank
            for t, base in ((tile, 0), (following, CAP))
        ]
        wanted = [w | ((window_of == j) & (slot_of == spot)) for w, spot in zip(wanted, spots)]
        shift = jnp.right_shift(probes[1, j], 2) - window // 2
        angle = turns(u * offset + v * shift, window)
        turn[0, j * share : (j + 1) * share, :] = jnp.cos(angle)
        turn[1, j * share : (j + 1) * share, :] = jnp.where(lane < kept, -jnp.sin(angle), jnp.sin(angle))
    same_line = iota(shape, 0) % share == iota(shape, 1) % share
    select[...] = jnp.where((wanted[0] | wanted[1]) & same_line, 1.0, 0.0).astype(bf16)

    for copy, chunk in zip(copies, chunks):
        copy.wait()
        flat = jnp.concatenate([smatrix[c, chunk].reshape(planes * window, window) for c in range(2)], axis=1)
        product = jnp.dot(flat, column_table[...], preferred_element_type=f32)
        spectra[chunk] = product.astype(bf16).reshape(planes, window, 2 * kept)


def chosen(lists, me_tile, window, n_tile):
    shape = (n_tile * PER_LIST, lists[0].shape[1])
    slot, item = iota(shape, 0), iota(shape, 1)
    rows = jnp.zeros(shape, i32)
    columns = jnp.zeros(shape, i32)
    for n, probes in enumerate(lists):
        here = slot // PER_LIST == n
        rows = jnp.where(here, probes[0:1, :], rows)
        columns = jnp.where(here, probes[1:2, :], columns)
    tile, _ = window_start(rows, window, window * n_tile)
    before = jnp.where(me_tile == 0, n_tile - 1, me_tile - 1)
    match = tile == jnp.where(slot % PER_LIST < CAP, me_tile, before)
    item = item.astype(f32)
    nothing = float(shape[1])
    left = jnp.where(match, item, nothing)
    picked = jnp.min(left, axis=1, keepdims=True)
    for n in range(1, CAP):
        left = jnp.where(left == picked, nothing, left)
        picked = jnp.where(slot[:, :1] % CAP >= n, jnp.min(left, axis=1, keepdims=True), picked)
    hit = item == picked
    return [jnp.sum(jnp.where(hit, x.astype(f32), 0.0), axis=1, keepdims=True) for x in (rows, columns)]


def parts_kernel(sizes, *refs):
    window, kept, n_tile, n_beam = sizes
    lists = in_order(refs[:n_tile], orders(n_tile)[0])
    beam_table, row_table, spectra, keep, send, coeff, waves = refs[n_tile:]
    share = kept // n_beam
    beams = spectra.shape[0]
    slots = n_tile * PER_LIST
    wide = beams * ROWS
    me_tile = lax.axis_index("tile")
    row_v, column_v = chosen(lists, me_tile, window, n_tile)
    offsets = jnp.bitwise_and(jnp.right_shift(row_v.astype(i32), 2) - window // 2, window - 1)
    offsets = jnp.broadcast_to(offsets, (slots, LANES))
    phase = beam_table[2:3, :] + two_pi / (window * IF) * (
        beam_table[0:1, :] * row_v + beam_table[1:2, :] * column_v
    )
    alpha = jnp.concatenate([jnp.cos(phase), -jnp.sin(phase)], axis=0).astype(bf16)
    spread = (iota((beams, wide), 1) // ROWS == iota((beams, wide), 0)).astype(f32).astype(bf16)
    alpha = jnp.dot(alpha, spread, preferred_element_type=f32)
    own_row = iota((ROWS, wide), 1) % ROWS == iota((ROWS, wide), 0)
    y_in = iota((ROWS, LANES), 0)
    lane = iota((kept, LANES), 1)
    sign = jnp.where(lane < kept, -1.0, 1.0)
    for first in range(0, slots, GROUP):
        for c in range(2):
            for p in range(GROUP):
                line = c * slots + first + p
                spot = (c * GROUP + p) * ROWS
                coeff[spot : spot + ROWS, :] = jnp.where(own_row, alpha[line : line + 1, :], 0.0).astype(bf16)
        for y in range(0, window, 2 * ROWS):
            pair = jnp.concatenate(
                [spectra[:, y + h : y + h + ROWS, :].reshape(wide, LANES) for h in (0, ROWS)], axis=1
            )
            made = jnp.dot(coeff[...], pair, preferred_element_type=f32)
            for h in range(2):
                y_here = y_in + (y + h * ROWS)
                for p in range(GROUP):
                    offset = offsets[first + p : first + p + 1, :]
                    starts_here = p % PER_LIST < CAP
                    inside = y_here >= offset if starts_here else y_here < offset
                    for c in range(2):
                        spot = (c * GROUP + p) * ROWS
                        value = made[spot : spot + ROWS, h * LANES : (h + 1) * LANES]
                        waves[c, p, y + h * ROWS : y + (h + 1) * ROWS, :] = jnp.where(inside, value, 0.0).astype(bf16)
        for p in range(0, GROUP, PER_LIST):
            fields = []
            for q in range(p, p + PER_LIST, 2):
                pair = jnp.concatenate(
                    [waves[:, q + h].reshape(2 * window, LANES) for h in range(2)], axis=1
                )
                both = jnp.dot(row_table[...], pair, preferred_element_type=f32)
                for h in range(2):
                    value = both[:, h * LANES : (h + 1) * LANES]
                    fields.append(value[:kept] + times_i(value[kept:]) * sign)
            k = (first + p) // PER_LIST
            for pos in range(n_beam):
                block = jnp.concatenate([f[pos * share : (pos + 1) * share] for f in fields], axis=0).astype(bf16)
                half = n_beam // 2
                if pos < half:
                    keep[pos, k] = block
                else:
                    send[pos - half, k] = block


def result_kernel(sizes, all_beams, *refs):
    window, kept, n_tile, n_beam = sizes
    turn, select = refs[:2]
    blocks = in_order(refs[2 : 2 + n_tile], orders(n_tile)[1])
    out, intensity = refs[2 + n_tile :]
    height = select.shape[0] // BIN
    shape = (2 * LANES, kept // BIN)
    bins = (iota(shape, 0) % kept // BIN == iota(shape, 1)).astype(f32).astype(bf16)
    arrived = jnp.concatenate([block[...] for block in blocks], axis=0)
    field = jnp.dot(select[...], arrived, preferred_element_type=f32)
    field = field * turn[0] + times_i(field) * turn[1]
    intensity[...] = field * field
    summed = intensity[pl.ds(0, height, stride=BIN), :]
    for b in range(1, BIN):
        summed = summed + intensity[pl.ds(b, height, stride=BIN), :]
    high = summed.astype(bf16)
    low = (summed - high.astype(f32)).astype(bf16)
    binned = jnp.dot(jnp.concatenate([high, low], axis=1), bins, preferred_element_type=f32)
    binned = binned * (1.0 / (BIN * BIN * window * window * all_beams))
    each = height // out.shape[0]
    for j in range(out.shape[0]):
        out[j] = binned[j * each : (j + 1) * each]


VMEM = pl.BlockSpec(memory_space=pltpu.VMEM)
HBM = pl.BlockSpec(memory_space=pltpu.HBM)


def params(mib=16):
    return pltpu.CompilerParams(vmem_limit_bytes=mib * 1024 * 1024)


def swapped(array, axis, by):
    return lax.ppermute(array, axis, [(i, i ^ by) for i in range(lax.axis_size(axis))])


def shifted(arrays, way, order):
    size = lax.axis_size("tile")
    return [
        lax.ppermute(arrays[k], "tile", [(i, (i + way * k) % size) for i in range(size)]) if k else arrays[0]
        for k in order
    ]


def in_order(refs, order):
    return [refs[order.index(k)] for k in range(len(order))]


def per_device(smatrix, beam_table, probes):
    _, beams, window, _ = smatrix.shape
    kept = window // 2
    n_tile = lax.axis_size("tile")
    n_beam = lax.axis_size("beam")
    sizes = (window, kept, n_tile, n_beam)
    share = kept // n_beam
    slots = n_tile * PER_LIST
    count = probes.shape[0]

    probes = probes.T
    lists_order, results_order = orders(n_tile)
    lists = shifted([probes] * n_tile, 1, lists_order)

    spectra, row_table, turn, select = pl.pallas_call(
        functools.partial(spectra_kernel, sizes),
        in_specs=[HBM, HBM],
        out_specs=[VMEM] * 4,
        out_shape=[
            jax.ShapeDtypeStruct((beams, window, 2 * kept), bf16),
            jax.ShapeDtypeStruct((2 * kept, 2 * window), bf16),
            jax.ShapeDtypeStruct((2, count * share, LANES), f32),
            jax.ShapeDtypeStruct((count * share, slots * share), bf16),
        ],
        scratch_shapes=[
            pltpu.VMEM((2 * window, 2 * kept), bf16),
            pltpu.VMEM(smatrix.shape, bf16),
            pltpu.SMEM(probes.shape, i32),
            pltpu.SemaphoreType.DMA((CHUNKS + 1,)),
        ],
        compiler_params=params(48),
        cost_estimate=pl.CostEstimate(
            flops=2 * beams * window * 4 * window * kept, bytes_accessed=smatrix.size * 3, transcendentals=0
        ),
        name="spectra",
    )(pltpu.with_memory_space_constraint(probes, pltpu.HBM), pltpu.with_memory_space_constraint(smatrix, pltpu.HBM))

    half = jax.ShapeDtypeStruct((n_beam // 2, n_tile, PER_LIST * share, LANES), bf16)
    keep, send = pl.pallas_call(
        functools.partial(parts_kernel, sizes),
        in_specs=[VMEM] * (n_tile + 3),
        out_specs=[VMEM] * 2,
        out_shape=[half, half],
        scratch_shapes=[
            pltpu.VMEM((2 * GROUP * ROWS, beams * ROWS), bf16),
            pltpu.VMEM((2, GROUP, window, LANES), bf16),
        ],
        compiler_params=params(),
        cost_estimate=pl.CostEstimate(
            flops=2 * slots * 2 * ROWS * beams * window * LANES, bytes_accessed=4 * 1024 * 1024, transcendentals=0
        ),
        name="parts",
    )(*lists, beam_table, row_table, spectra)

    by = 1
    while by < n_beam:
        arrived = swapped(send, "beam", by)
        total = (keep.astype(f32) + arrived.astype(f32)).astype(bf16)
        by *= 2
        middle = total.shape[0] // 2
        keep, send = total[:middle], total[middle:]
    mine = total[0]
    blocks = shifted(mine, -1, results_order)

    return pl.pallas_call(
        functools.partial(result_kernel, sizes, beams * n_beam),
        in_specs=[VMEM] * (2 + n_tile),
        out_specs=VMEM,
        out_shape=jax.ShapeDtypeStruct((count, share // BIN, kept // BIN), f32),
        scratch_shapes=[pltpu.VMEM((count * share, LANES), f32)],
        compiler_params=params(),
        name="result",
    )(turn, select, *blocks)


def solution(mesh):
    in_specs = (
        P(None, ("groups", "beam"), "tile", None),
        P(None, "beam"),
        P(("groups", "tile"), None),
    )
    out_specs = P(("groups", "tile"), "beam", None)
    return jax.shard_map(
        per_device, mesh=mesh, in_specs=in_specs, out_specs=out_specs, check_vma=False
    )
```

```python
import functools
import math

import jax
import jax.numpy as jnp
from jax import lax
from jax.experimental import pallas as pl
from jax.experimental.pallas import tpu as pltpu
from jax.sharding import PartitionSpec as P

IF = 4
BIN = 2
CAP = 2
PER_LIST = 2 * CAP
LANES = 128
GROUP = 8
CHUNKS = 1
ROWS = 16

LISTS_ORDER = (0, 1, 3, 2)
RESULTS_ORDER = (0, 1, 3, 2)


def orders(n_tile):
    if n_tile == 4:
        return LISTS_ORDER, RESULTS_ORDER
    return tuple(range(n_tile)), tuple(range(n_tile))


two_pi = 2.0 * math.pi
f32 = jnp.float32
bf16 = jnp.bfloat16
i32 = jnp.int32


def iota(shape, dim):
    return lax.broadcasted_iota(i32, shape, dim)


def series(square, last):
    total = jnp.full_like(square, (-1.0) ** (last // 2) / math.factorial(last))
    for n in range(last - 2, -1, -2):
        total = total * square + (-1.0) ** (n // 2) / math.factorial(n)
    return total


def cos_sin(turn):
    x = (turn - jnp.floor(turn + 0.5)) * two_pi
    square = x * x
    return series(square, 18), series(square, 19) * x


def angle_of(index, window):
    half = window // 2
    return (two_pi / window) * (jnp.bitwise_and(index + half, window - 1) - half).astype(f32)


def cosine_of(index, window):
    angle = angle_of(index, window)
    return series(angle * angle, 18)


def bit_reversed(number, count):
    bits = count.bit_length() - 1
    return sum(((number >> b) & 1) << (bits - 1 - b) for b in range(bits))


def window_start(row, window, field_rows):
    start = jnp.right_shift(row, 2) - window // 2
    start = jnp.where(start < 0, start + field_rows, start)
    tile = jnp.right_shift(start, window.bit_length() - 1)
    return tile, jnp.bitwise_and(start, window - 1)


def times_i(pairs):
    return pltpu.roll(pairs, LANES // 2, pairs.ndim - 1)


def spectra_kernel(
    sizes, probes_hbm, smatrix_hbm, table_hbm, spectra, row_table, turn, select, beam_turns, *scratch
):
    window, kept, n_tile, n_beam = sizes
    share = kept // n_beam
    me_beam = lax.axis_index("beam")
    me_tile = lax.axis_index("tile")
    column_table, smatrix, probes, beam_table, sems = scratch
    planes = smatrix.shape[1] // CHUNKS
    chunks = [pl.ds(i * planes, planes) for i in range(CHUNKS)]
    copies = [
        pltpu.make_async_copy(smatrix_hbm.at[:, chunk], smatrix.at[:, chunk], sems.at[i])
        for i, chunk in enumerate(chunks)
    ]
    for copy in copies:
        copy.start()
    listed = pltpu.make_async_copy(probes_hbm, probes, sems.at[CHUNKS])
    listed.start()
    tabled = pltpu.make_async_copy(table_hbm, beam_table, sems.at[CHUNKS + 1])
    tabled.start()

    shape = (2 * window, 2 * kept)
    x, part_in = iota(shape, 0) % window, iota(shape, 0) // window
    lane = iota(shape, 1)
    v, part_out = lane % kept - kept // 2, lane // kept
    index = x * v + (window // 4) * (part_out - part_in)
    column_table[...] = cosine_of(index, window).astype(bf16)

    shape = (2 * kept, 2 * window)
    line, turned = iota(shape, 0) % kept, iota(shape, 0) // kept
    r, part_in = iota(shape, 1) % window, iota(shape, 1) // window
    block = line // share
    owner = jnp.zeros_like(block)
    for pos in range(n_beam):
        owner = jnp.where(block == pos, jnp.bitwise_xor(me_beam, bit_reversed(pos, n_beam)), owner)
    u = owner * share + line % share - kept // 2
    index = u * r + (window // 4) * (turned - part_in)
    row_table[...] = cosine_of(index, window).astype(bf16)

    u = iota((share, LANES), 0) + me_beam * share - kept // 2
    lane = iota((share, LANES), 1)
    v = lane % kept - kept // 2
    tabled.wait()
    beams, wide = beam_table.shape[1], beam_turns.shape[1]
    spread = (iota((beams, wide), 1) // ROWS == iota((beams, wide), 0)).astype(f32)
    wave_numbers = beam_table[...]
    scale = jnp.where(iota(wave_numbers.shape, 0) < 2, 1.0 / (window * IF), 1.0 / two_pi)
    beam_turns[...] = jnp.dot(
        wave_numbers * scale, spread, precision=lax.Precision.HIGHEST, preferred_element_type=f32
    )

    listed.wait()
    shape = (select.shape[0], select.shape[1])
    window_of, slot_of = iota(shape, 0) // share, iota(shape, 1) // share
    wanted = (slot_of == -1, slot_of == -1)
    tiles = []
    for j in range(probes.shape[1]):
        tile, offset = window_start(probes[0, j], window, window * n_tile)
        following = jnp.where(tile == n_tile - 1, 0, tile + 1)
        rank = sum([(t == tile).astype(i32) for t in tiles], i32(0))
        tiles.append(tile)
        spots = [
            (jnp.where(t < me_tile, t + n_tile, t) - me_tile) * PER_LIST + base + rank
            for t, base in ((tile, 0), (following, CAP))
        ]
        wanted = [w | ((window_of == j) & (slot_of == spot)) for w, spot in zip(wanted, spots)]
        shift = jnp.right_shift(probes[1, j], 2) - window // 2
        angle = angle_of(u * offset + v * shift, window)
        square = angle * angle
        turn[0, j * share : (j + 1) * share, :] = series(square, 18)
        turn[1, j * share : (j + 1) * share, :] = series(square, 19) * jnp.where(lane < kept, -angle, angle)
    same_line = iota(shape, 0) % share == iota(shape, 1) % share
    select[...] = jnp.where((wanted[0] | wanted[1]) & same_line, 1.0, 0.0).astype(bf16)

    for copy, chunk in zip(copies, chunks):
        copy.wait()
        flat = jnp.concatenate([smatrix[c, chunk].reshape(planes * window, window) for c in range(2)], axis=1)
        product = jnp.dot(flat, column_table[...], preferred_element_type=f32)
        spectra[chunk] = product.astype(bf16).reshape(planes, window, 2 * kept)


def chosen(lists, me_tile, window, n_tile):
    shape = (len(lists) * PER_LIST, lists[0].shape[1])
    slot, item = iota(shape, 0), iota(shape, 1)
    rows = jnp.zeros(shape, i32)
    columns = jnp.zeros(shape, i32)
    for n, probes in enumerate(lists):
        here = slot // PER_LIST == n
        rows = jnp.where(here, probes[0:1, :], rows)
        columns = jnp.where(here, probes[1:2, :], columns)
    tile, _ = window_start(rows, window, window * n_tile)
    before = jnp.where(me_tile == 0, n_tile - 1, me_tile - 1)
    match = tile == jnp.where(slot % PER_LIST < CAP, me_tile, before)
    item = item.astype(f32)
    nothing = float(shape[1])
    left = jnp.where(match, item, nothing)
    picked = jnp.min(left, axis=1, keepdims=True)
    for n in range(1, CAP):
        left = jnp.where(left == picked, nothing, left)
        picked = jnp.where(slot[:, :1] % CAP >= n, jnp.min(left, axis=1, keepdims=True), picked)
    hit = item == picked
    return [jnp.sum(jnp.where(hit, x.astype(f32), 0.0), axis=1, keepdims=True) for x in (rows, columns)]


def coefficients_kernel(sizes, *refs):
    window, kept, n_tile, n_beam = sizes
    lists, (beam_turns, row_table, spectra, keep, send, later, later_offsets, coeff, waves) = refs[:-9], refs[-9:]
    slots = len(lists) * PER_LIST
    wide = beam_turns.shape[1]
    now = keep.shape[1] * PER_LIST
    me_tile = lax.axis_index("tile")
    row_v, column_v = chosen(lists, me_tile, window, n_tile)
    offsets = jnp.bitwise_and(jnp.right_shift(row_v.astype(i32), 2) - window // 2, window - 1)
    offsets = jnp.broadcast_to(offsets, (slots, LANES))
    later_offsets[...] = offsets[now:]
    alpha_re, alpha_im = cos_sin(
        beam_turns[2:3, :] + (beam_turns[0:1, :] * row_v + beam_turns[1:2, :] * column_v)
    )
    own_row = iota((ROWS, wide), 1) % ROWS == iota((ROWS, wide), 0)
    for c, alpha in enumerate((alpha_re, -alpha_im)):
        for p in range(slots):
            line = jnp.where(own_row, alpha[p : p + 1, :], 0.0).astype(bf16)
            if p < now:
                coeff[p // GROUP, c, p % GROUP] = line
            else:
                later[(p - now) // GROUP, c, (p - now) % GROUP] = line
    make_parts(sizes, coeff, offsets[:now], row_table, spectra, keep, send, waves)


def parts_kernel(sizes, coeff, offsets, row_table, spectra, keep, send, waves):
    make_parts(sizes, coeff, offsets[...], row_table, spectra, keep, send, waves)


def make_parts(sizes, coeff, offsets, row_table, spectra, keep, send, waves):
    window, kept, n_tile, n_beam = sizes
    share = kept // n_beam
    wide = spectra.shape[0] * ROWS
    y_in = iota((ROWS, LANES), 0)
    lane = iota((kept, LANES), 1)
    sign = jnp.where(lane < kept, -1.0, 1.0)
    for group in range(coeff.shape[0]):
        first = group * GROUP
        matrix = coeff[group].reshape(2 * GROUP * ROWS, wide)
        for y in range(0, window, 2 * ROWS):
            pair = jnp.concatenate(
                [spectra[:, y + h : y + h + ROWS, :].reshape(wide, LANES) for h in (0, ROWS)], axis=1
            )
            made = jnp.dot(matrix, pair, preferred_element_type=f32)
            for h in range(2):
                y_here = y_in + (y + h * ROWS)
                for p in range(GROUP):
                    offset = offsets[first + p : first + p + 1, :]
                    starts_here = p % PER_LIST < CAP
                    inside = y_here >= offset if starts_here else y_here < offset
                    for c in range(2):
                        spot = (c * GROUP + p) * ROWS
                        value = made[spot : spot + ROWS, h * LANES : (h + 1) * LANES]
                        waves[c, p, y + h * ROWS : y + (h + 1) * ROWS, :] = jnp.where(inside, value, 0.0).astype(bf16)
        for p in range(0, GROUP, PER_LIST):
            fields = []
            for q in range(p, p + PER_LIST, 2):
                pair = jnp.concatenate(
                    [waves[:, q + h].reshape(2 * window, LANES) for h in range(2)], axis=1
                )
                both = jnp.dot(row_table[...], pair, preferred_element_type=f32)
                for h in range(2):
                    value = both[:, h * LANES : (h + 1) * LANES]
                    fields.append(value[:kept] + times_i(value[kept:]) * sign)
            k = (first + p) // PER_LIST
            for pos in range(n_beam):
                block = jnp.concatenate([f[pos * share : (pos + 1) * share] for f in fields], axis=0).astype(bf16)
                half = n_beam // 2
                if pos < half:
                    keep[pos, k] = block
                else:
                    send[pos - half, k] = block


def result_kernel(sizes, all_beams, *refs):
    window, kept, n_tile, n_beam = sizes
    turn, select = refs[:2]
    blocks = in_order(refs[2 : 2 + n_tile], orders(n_tile)[1])
    out, intensity = refs[2 + n_tile :]
    height = select.shape[0] // BIN
    shape = (2 * LANES, kept // BIN)
    bins = (iota(shape, 0) % kept // BIN == iota(shape, 1)).astype(f32).astype(bf16)
    arrived = jnp.concatenate([block[...] for block in blocks], axis=0)
    field = jnp.dot(select[...], arrived, preferred_element_type=f32)
    field = field * turn[0] + times_i(field) * turn[1]
    intensity[...] = field * field
    summed = intensity[pl.ds(0, height, stride=BIN), :]
    for b in range(1, BIN):
        summed = summed + intensity[pl.ds(b, height, stride=BIN), :]
    high = summed.astype(bf16)
    low = (summed - high.astype(f32)).astype(bf16)
    binned = jnp.dot(jnp.concatenate([high, low], axis=1), bins, preferred_element_type=f32)
    binned = binned * (1.0 / (BIN * BIN * window * window * all_beams))
    each = height // out.shape[0]
    for j in range(out.shape[0]):
        out[j] = binned[j * each : (j + 1) * each]


VMEM = pl.BlockSpec(memory_space=pltpu.VMEM)
HBM = pl.BlockSpec(memory_space=pltpu.HBM)


def params(mib=16):
    return pltpu.CompilerParams(vmem_limit_bytes=mib * 1024 * 1024)


def swapped(array, axis, by):
    return lax.ppermute(array, axis, [(i, i ^ by) for i in range(lax.axis_size(axis))])


def shifted(arrays, way, order):
    size = lax.axis_size("tile")
    return [
        lax.ppermute(arrays[k], "tile", [(i, (i + way * k) % size) for i in range(size)]) if k else arrays[0]
        for k in order
    ]


def halves(n_tile):
    numbers = list(range(n_tile))[::-1]
    return numbers[: n_tile // 2], numbers[n_tile // 2 :]


def in_order(refs, order):
    return [refs[order.index(k)] for k in range(len(order))]


def per_device(smatrix, beam_table, probes):
    _, beams, window, _ = smatrix.shape
    kept = window // 2
    n_tile = lax.axis_size("tile")
    n_beam = lax.axis_size("beam")
    sizes = (window, kept, n_tile, n_beam)
    share = kept // n_beam
    slots = n_tile * PER_LIST
    count = probes.shape[0]

    probes = probes.T
    lists_order, results_order = orders(n_tile)
    lists = lax.optimization_barrier(shifted([probes] * n_tile, 1, lists_order))
    lists = dict(zip(lists_order, lists))

    spectra, row_table, turn, select, beam_turns = pl.pallas_call(
        functools.partial(spectra_kernel, sizes),
        in_specs=[HBM, HBM, HBM],
        out_specs=[VMEM] * 5,
        out_shape=[
            jax.ShapeDtypeStruct((beams, window, 2 * kept), bf16),
            jax.ShapeDtypeStruct((2 * kept, 2 * window), bf16),
            jax.ShapeDtypeStruct((2, count * share, LANES), f32),
            jax.ShapeDtypeStruct((count * share, slots * share), bf16),
            jax.ShapeDtypeStruct((3, beams * ROWS), f32),
        ],
        scratch_shapes=[
            pltpu.VMEM((2 * window, 2 * kept), bf16),
            pltpu.VMEM(smatrix.shape, bf16),
            pltpu.SMEM(probes.shape, i32),
            pltpu.VMEM(beam_table.shape, f32),
            pltpu.SemaphoreType.DMA((CHUNKS + 2,)),
        ],
        compiler_params=params(48),
        cost_estimate=pl.CostEstimate(
            flops=2 * beams * window * 4 * window * kept, bytes_accessed=smatrix.size * 3, transcendentals=0
        ),
        name="spectra",
    )(
        pltpu.with_memory_space_constraint(probes, pltpu.HBM),
        pltpu.with_memory_space_constraint(smatrix, pltpu.HBM),
        pltpu.with_memory_space_constraint(beam_table, pltpu.HBM),
    )

    earlier, later = halves(n_tile)

    def parts_call(kernel, numbers, operands, more, scratch, name):
        half = jax.ShapeDtypeStruct((n_beam // 2, len(numbers), PER_LIST * share, LANES), bf16)
        return pl.pallas_call(
            functools.partial(kernel, sizes),
            in_specs=[VMEM] * len(operands),
            out_specs=[VMEM] * (2 + len(more)),
            out_shape=[half, half, *more],
            scratch_shapes=[*scratch, pltpu.VMEM((2, GROUP, window, LANES), bf16)],
            compiler_params=params(),
            cost_estimate=pl.CostEstimate(
                flops=2 * len(numbers) * PER_LIST * 2 * ROWS * beams * window * LANES,
                bytes_accessed=4 * 1024 * 1024,
                transcendentals=0,
            ),
            name=name,
        )(*operands)

    coeff_shape = (len(earlier) * PER_LIST // GROUP, 2, GROUP, ROWS, beams * ROWS)
    keep, send, coeff, offsets = parts_call(
        coefficients_kernel,
        earlier,
        [lists[n] for n in earlier + later] + [beam_turns, row_table, spectra],
        [
            jax.ShapeDtypeStruct(coeff_shape, bf16),
            jax.ShapeDtypeStruct((len(later) * PER_LIST, LANES), i32),
        ],
        [pltpu.VMEM(coeff_shape, bf16)],
        "coefficients",
    )
    halves_made = [
        (earlier, keep, send),
        (later, *parts_call(parts_kernel, later, [coeff, offsets, row_table, spectra], [], [], "parts")),
    ]

    results = {}
    for numbers, keep, send in halves_made:
        by = 1
        while by < n_beam:
            arrived = swapped(send, "beam", by)
            total = (keep.astype(f32) + arrived.astype(f32)).astype(bf16)
            by *= 2
            middle = total.shape[0] // 2
            keep, send = total[:middle], total[middle:]
        results |= {n: total[0, i] for i, n in enumerate(numbers)}
    blocks = shifted(results, -1, results_order)

    return pl.pallas_call(
        functools.partial(result_kernel, sizes, beams * n_beam),
        in_specs=[VMEM] * (2 + n_tile),
        out_specs=VMEM,
        out_shape=jax.ShapeDtypeStruct((count, share // BIN, kept // BIN), f32),
        scratch_shapes=[pltpu.VMEM((count * share, LANES), f32)],
        compiler_params=params(),
        name="result",
    )(turn, select, *blocks)


def solution(mesh):
    in_specs = (
        P(None, ("groups", "beam"), "tile", None),
        P(None, "beam"),
        P(("groups", "tile"), None),
    )
    out_specs = P(("groups", "tile"), "beam", None)
    return jax.shard_map(
        per_device, mesh=mesh, in_specs=in_specs, out_specs=out_specs, check_vma=False
    )
```

```python
import functools
import math

import jax
import jax.numpy as jnp
from jax import lax
from jax.experimental import pallas as pl
from jax.experimental.pallas import tpu as pltpu
from jax.sharding import PartitionSpec as P

IF = 4
BIN = 2
CAP = 2
PER_LIST = 2 * CAP
LANES = 128
GROUP = 8
CHUNKS = 1
ROWS = 8

LISTS_ORDER = (0, 1, 3, 2)
RESULTS_ORDER = (0, 1, 3, 2)


def orders(n_tile):
    if n_tile == 4:
        return LISTS_ORDER, RESULTS_ORDER
    return tuple(range(n_tile)), tuple(range(n_tile))


two_pi = 2.0 * math.pi
f32 = jnp.float32
bf16 = jnp.bfloat16
i32 = jnp.int32


def iota(shape, dim):
    return lax.broadcasted_iota(i32, shape, dim)


def series(square, last):
    total = jnp.full_like(square, (-1.0) ** (last // 2) / math.factorial(last))
    for n in range(last - 2, -1, -2):
        total = total * square + (-1.0) ** (n // 2) / math.factorial(n)
    return total


def cos_sin(turn):
    x = (turn - jnp.floor(turn + 0.5)) * two_pi
    square = x * x
    return series(square, 18), series(square, 19) * x


def angle_of(index, window):
    half = window // 2
    return (two_pi / window) * (jnp.bitwise_and(index + half, window - 1) - half).astype(f32)


def cosine_of(index, window):
    angle = angle_of(index, window)
    return series(angle * angle, 18)


def bit_reversed(number, count):
    bits = count.bit_length() - 1
    return sum(((number >> b) & 1) << (bits - 1 - b) for b in range(bits))


def window_start(row, window, field_rows):
    start = jnp.right_shift(row, 2) - window // 2
    start = jnp.where(start < 0, start + field_rows, start)
    tile = jnp.right_shift(start, window.bit_length() - 1)
    return tile, jnp.bitwise_and(start, window - 1)


def times_i(pairs):
    return pltpu.roll(pairs, LANES // 2, pairs.ndim - 1)


def spectra_kernel(
    sizes, probes_hbm, smatrix_hbm, table_hbm, spectra, row_table, turn, select, beam_turns, *scratch
):
    window, kept, n_tile, n_beam = sizes
    share = kept // n_beam
    me_beam = lax.axis_index("beam")
    me_tile = lax.axis_index("tile")
    column_table, smatrix, probes, beam_table, sems = scratch
    planes = smatrix.shape[1] // CHUNKS
    chunks = [pl.ds(i * planes, planes) for i in range(CHUNKS)]
    copies = [
        pltpu.make_async_copy(smatrix_hbm.at[:, chunk], smatrix.at[:, chunk], sems.at[i])
        for i, chunk in enumerate(chunks)
    ]
    for copy in copies:
        copy.start()
    listed = pltpu.make_async_copy(probes_hbm, probes, sems.at[CHUNKS])
    listed.start()
    tabled = pltpu.make_async_copy(table_hbm, beam_table, sems.at[CHUNKS + 1])
    tabled.start()

    shape = (2 * window, 2 * kept)
    x, part_in = iota(shape, 0) % window, iota(shape, 0) // window
    lane = iota(shape, 1)
    v, part_out = lane % kept - kept // 2, lane // kept
    index = x * v + (window // 4) * (part_out - part_in)
    column_table[...] = cosine_of(index, window).astype(bf16)

    shape = (2 * kept, 2 * window)
    line, turned = iota(shape, 0) % kept, iota(shape, 0) // kept
    r, part_in = iota(shape, 1) % window, iota(shape, 1) // window
    block = line // share
    owner = jnp.zeros_like(block)
    for pos in range(n_beam):
        owner = jnp.where(block == pos, jnp.bitwise_xor(me_beam, bit_reversed(pos, n_beam)), owner)
    u = owner * share + line % share - kept // 2
    index = u * r + (window // 4) * (turned - part_in)
    row_table[...] = cosine_of(index, window).astype(bf16)

    u = iota((share, LANES), 0) + me_beam * share - kept // 2
    lane = iota((share, LANES), 1)
    v = lane % kept - kept // 2
    tabled.wait()
    beams, wide = beam_table.shape[1], beam_turns.shape[1]
    spread = (iota((beams, wide), 1) // ROWS == iota((beams, wide), 0)).astype(f32)
    wave_numbers = beam_table[...]
    scale = jnp.where(iota(wave_numbers.shape, 0) < 2, 1.0 / (window * IF), 1.0 / two_pi)
    beam_turns[...] = jnp.dot(
        wave_numbers * scale, spread, precision=lax.Precision.HIGHEST, preferred_element_type=f32
    )

    listed.wait()
    shape = (select.shape[0], select.shape[1])
    window_of, slot_of = iota(shape, 0) // share, iota(shape, 1) // share
    wanted = (slot_of == -1, slot_of == -1)
    tiles = []
    for j in range(probes.shape[1]):
        tile, offset = window_start(probes[0, j], window, window * n_tile)
        following = jnp.where(tile == n_tile - 1, 0, tile + 1)
        rank = sum([(t == tile).astype(i32) for t in tiles], i32(0))
        tiles.append(tile)
        spots = [
            (jnp.where(t < me_tile, t + n_tile, t) - me_tile) * PER_LIST + base + rank
            for t, base in ((tile, 0), (following, CAP))
        ]
        wanted = [w | ((window_of == j) & (slot_of == spot)) for w, spot in zip(wanted, spots)]
        shift = jnp.right_shift(probes[1, j], 2) - window // 2
        angle = angle_of(u * offset + v * shift, window)
        square = angle * angle
        turn[0, j * share : (j + 1) * share, :] = series(square, 18)
        turn[1, j * share : (j + 1) * share, :] = series(square, 19) * jnp.where(lane < kept, -angle, angle)
    same_line = iota(shape, 0) % share == iota(shape, 1) % share
    select[...] = jnp.where((wanted[0] | wanted[1]) & same_line, 1.0, 0.0).astype(bf16)

    for i, (copy, chunk) in enumerate(zip(copies, chunks)):
        copy.wait()
        flat = jnp.concatenate([smatrix[c, chunk].reshape(planes * window, window) for c in range(2)], axis=1)
        product = jnp.dot(flat, column_table[...], preferred_element_type=f32)
        product = product.reshape(planes, window // ROWS, ROWS, 2 * kept)
        for t in range(window // ROWS):
            rows = slice(i * planes * ROWS, (i + 1) * planes * ROWS)
            spectra[t, rows, :] = product[:, t].reshape(planes * ROWS, 2 * kept).astype(bf16)


def chosen(lists, me_tile, window, n_tile):
    shape = (len(lists) * PER_LIST, lists[0].shape[1])
    slot, item = iota(shape, 0), iota(shape, 1)
    rows = jnp.zeros(shape, i32)
    columns = jnp.zeros(shape, i32)
    for n, probes in enumerate(lists):
        here = slot // PER_LIST == n
        rows = jnp.where(here, probes[0:1, :], rows)
        columns = jnp.where(here, probes[1:2, :], columns)
    tile, _ = window_start(rows, window, window * n_tile)
    before = jnp.where(me_tile == 0, n_tile - 1, me_tile - 1)
    match = tile == jnp.where(slot % PER_LIST < CAP, me_tile, before)
    item = item.astype(f32)
    nothing = float(shape[1])
    left = jnp.where(match, item, nothing)
    picked = jnp.min(left, axis=1, keepdims=True)
    for n in range(1, CAP):
        left = jnp.where(left == picked, nothing, left)
        picked = jnp.where(slot[:, :1] % CAP >= n, jnp.min(left, axis=1, keepdims=True), picked)
    hit = item == picked
    return [jnp.sum(jnp.where(hit, x.astype(f32), 0.0), axis=1, keepdims=True) for x in (rows, columns)]


def coefficients_kernel(sizes, *refs):
    window, kept, n_tile, n_beam = sizes
    lists, (beam_turns, row_table, spectra, keep, send, later, later_offsets, coeff, waves) = refs[:-9], refs[-9:]
    slots = len(lists) * PER_LIST
    wide = beam_turns.shape[1]
    now = keep.shape[1] * PER_LIST
    me_tile = lax.axis_index("tile")
    row_v, column_v = chosen(lists, me_tile, window, n_tile)
    offsets = jnp.bitwise_and(jnp.right_shift(row_v.astype(i32), 2) - window // 2, window - 1)
    offsets = jnp.broadcast_to(offsets, (slots, LANES))
    later_offsets[...] = offsets[now:]
    alpha_re, alpha_im = cos_sin(
        beam_turns[2:3, :] + (beam_turns[0:1, :] * row_v + beam_turns[1:2, :] * column_v)
    )
    pair = iota((2 * ROWS, wide), 0)
    own_row = iota((2 * ROWS, wide), 1) % ROWS == pair % ROWS
    for c, alpha in enumerate((alpha_re, -alpha_im)):
        for p in range(0, slots, 2):
            lines = jnp.where(pair < ROWS, alpha[p : p + 1, :], alpha[p + 1 : p + 2, :])
            lines = jnp.where(own_row, lines, 0.0).astype(bf16)
            if p < now:
                coeff[p // GROUP, c, p % GROUP // 2] = lines
            else:
                later[(p - now) // GROUP, c, (p - now) % GROUP // 2] = lines
    make_parts(sizes, coeff, offsets[:now], row_table, spectra, keep, send, waves)


def parts_kernel(sizes, coeff, offsets, row_table, spectra, keep, send, waves):
    make_parts(sizes, coeff, offsets[...], row_table, spectra, keep, send, waves)


def make_parts(sizes, coeff, offsets, row_table, spectra, keep, send, waves):
    window, kept, n_tile, n_beam = sizes
    share = kept // n_beam
    y_in = iota((2 * ROWS, LANES), 0)
    lane = iota((kept, LANES), 1)
    sign = jnp.where(lane < kept, -1.0, 1.0)
    for group in range(coeff.shape[0]):
        first = group * GROUP
        matrix = coeff[group].reshape(2 * GROUP * ROWS, spectra.shape[1])
        for t in range(0, spectra.shape[0], 2):
            pair = jnp.concatenate([spectra[t], spectra[t + 1]], axis=1)
            made = jnp.dot(matrix, pair, preferred_element_type=f32)
            y = t * ROWS
            for p in range(GROUP):
                offset = offsets[first + p : first + p + 1, :]
                starts_here = p % PER_LIST < CAP
                inside = y_in + y >= offset if starts_here else y_in + y < offset
                for c in range(2):
                    spot = (c * GROUP + p) * ROWS
                    value = made[spot : spot + ROWS, :]
                    value = jnp.concatenate([value[:, :LANES], value[:, LANES:]], axis=0)
                    waves[c, p, y : y + 2 * ROWS, :] = jnp.where(inside, value, 0.0).astype(bf16)
        for p in range(0, GROUP, PER_LIST):
            fields = []
            for q in range(p, p + PER_LIST, 2):
                pair = jnp.concatenate(
                    [waves[:, q + h].reshape(2 * window, LANES) for h in range(2)], axis=1
                )
                both = jnp.dot(row_table[...], pair, preferred_element_type=f32)
                for h in range(2):
                    value = both[:, h * LANES : (h + 1) * LANES]
                    fields.append(value[:kept] + times_i(value[kept:]) * sign)
            k = (first + p) // PER_LIST
            for pos in range(n_beam):
                block = jnp.concatenate([f[pos * share : (pos + 1) * share] for f in fields], axis=0).astype(bf16)
                half = n_beam // 2
                if pos < half:
                    keep[pos, k] = block
                else:
                    send[pos - half, k] = block


def result_kernel(sizes, all_beams, *refs):
    window, kept, n_tile, n_beam = sizes
    turn, select = refs[:2]
    blocks = in_order(refs[2 : 2 + n_tile], orders(n_tile)[1])
    out, intensity = refs[2 + n_tile :]
    height = select.shape[0] // BIN
    shape = (2 * LANES, kept // BIN)
    bins = (iota(shape, 0) % kept // BIN == iota(shape, 1)).astype(f32).astype(bf16)
    arrived = jnp.concatenate([block[...] for block in blocks], axis=0)
    field = jnp.dot(select[...], arrived, preferred_element_type=f32)
    field = field * turn[0] + times_i(field) * turn[1]
    intensity[...] = field * field
    summed = intensity[pl.ds(0, height, stride=BIN), :]
    for b in range(1, BIN):
        summed = summed + intensity[pl.ds(b, height, stride=BIN), :]
    high = summed.astype(bf16)
    low = (summed - high.astype(f32)).astype(bf16)
    binned = jnp.dot(jnp.concatenate([high, low], axis=1), bins, preferred_element_type=f32)
    binned = binned * (1.0 / (BIN * BIN * window * window * all_beams))
    each = height // out.shape[0]
    for j in range(out.shape[0]):
        out[j] = binned[j * each : (j + 1) * each]


VMEM = pl.BlockSpec(memory_space=pltpu.VMEM)
HBM = pl.BlockSpec(memory_space=pltpu.HBM)


def params(mib=16):
    return pltpu.CompilerParams(vmem_limit_bytes=mib * 1024 * 1024)


def swapped(array, axis, by):
    return lax.ppermute(array, axis, [(i, i ^ by) for i in range(lax.axis_size(axis))])


def shifted(arrays, way, order):
    size = lax.axis_size("tile")
    return [
        lax.ppermute(arrays[k], "tile", [(i, (i + way * k) % size) for i in range(size)]) if k else arrays[0]
        for k in order
    ]


def halves(n_tile):
    numbers = list(range(n_tile))[::-1]
    return numbers[: n_tile // 2], numbers[n_tile // 2 :]


def in_order(refs, order):
    return [refs[order.index(k)] for k in range(len(order))]


def per_device(smatrix, beam_table, probes):
    _, beams, window, _ = smatrix.shape
    kept = window // 2
    n_tile = lax.axis_size("tile")
    n_beam = lax.axis_size("beam")
    sizes = (window, kept, n_tile, n_beam)
    share = kept // n_beam
    slots = n_tile * PER_LIST
    count = probes.shape[0]

    probes = probes.T
    lists_order, results_order = orders(n_tile)
    lists = lax.optimization_barrier(shifted([probes] * n_tile, 1, lists_order))
    lists = dict(zip(lists_order, lists))

    spectra, row_table, turn, select, beam_turns = pl.pallas_call(
        functools.partial(spectra_kernel, sizes),
        in_specs=[HBM, HBM, HBM],
        out_specs=[VMEM] * 5,
        out_shape=[
            jax.ShapeDtypeStruct((window // ROWS, beams * ROWS, 2 * kept), bf16),
            jax.ShapeDtypeStruct((2 * kept, 2 * window), bf16),
            jax.ShapeDtypeStruct((2, count * share, LANES), f32),
            jax.ShapeDtypeStruct((count * share, slots * share), bf16),
            jax.ShapeDtypeStruct((3, beams * ROWS), f32),
        ],
        scratch_shapes=[
            pltpu.VMEM((2 * window, 2 * kept), bf16),
            pltpu.VMEM(smatrix.shape, bf16),
            pltpu.SMEM(probes.shape, i32),
            pltpu.VMEM(beam_table.shape, f32),
            pltpu.SemaphoreType.DMA((CHUNKS + 2,)),
        ],
        compiler_params=params(48),
        cost_estimate=pl.CostEstimate(
            flops=2 * beams * window * 4 * window * kept, bytes_accessed=smatrix.size * 3, transcendentals=0
        ),
        name="spectra",
    )(
        pltpu.with_memory_space_constraint(probes, pltpu.HBM),
        pltpu.with_memory_space_constraint(smatrix, pltpu.HBM),
        pltpu.with_memory_space_constraint(beam_table, pltpu.HBM),
    )

    earlier, later = halves(n_tile)

    def parts_call(kernel, numbers, operands, more, scratch, name):
        half = jax.ShapeDtypeStruct((n_beam // 2, len(numbers), PER_LIST * share, LANES), bf16)
        return pl.pallas_call(
            functools.partial(kernel, sizes),
            in_specs=[VMEM] * len(operands),
            out_specs=[VMEM] * (2 + len(more)),
            out_shape=[half, half, *more],
            scratch_shapes=[*scratch, pltpu.VMEM((2, GROUP, window, LANES), bf16)],
            compiler_params=params(),
            cost_estimate=pl.CostEstimate(
                flops=2 * len(numbers) * PER_LIST * 2 * ROWS * beams * window * LANES,
                bytes_accessed=4 * 1024 * 1024,
                transcendentals=0,
            ),
            name=name,
        )(*operands)

    coeff_shape = (len(earlier) * PER_LIST // GROUP, 2, GROUP // 2, 2 * ROWS, beams * ROWS)
    keep, send, coeff, offsets = parts_call(
        coefficients_kernel,
        earlier,
        [lists[n] for n in earlier + later] + [beam_turns, row_table, spectra],
        [
            jax.ShapeDtypeStruct(coeff_shape, bf16),
            jax.ShapeDtypeStruct((len(later) * PER_LIST, LANES), i32),
        ],
        [pltpu.VMEM(coeff_shape, bf16)],
        "coefficients",
    )
    halves_made = [
        (earlier, keep, send),
        (later, *parts_call(parts_kernel, later, [coeff, offsets, row_table, spectra], [], [], "parts")),
    ]

    results = {}
    for numbers, keep, send in halves_made:
        by = 1
        while by < n_beam:
            arrived = swapped(send, "beam", by)
            total = (keep.astype(f32) + arrived.astype(f32)).astype(bf16)
            by *= 2
            middle = total.shape[0] // 2
            keep, send = total[:middle], total[middle:]
        results |= {n: total[0, i] for i, n in enumerate(numbers)}
    blocks = shifted(results, -1, results_order)

    return pl.pallas_call(
        functools.partial(result_kernel, sizes, beams * n_beam),
        in_specs=[VMEM] * (2 + n_tile),
        out_specs=VMEM,
        out_shape=jax.ShapeDtypeStruct((count, share // BIN, kept // BIN), f32),
        scratch_shapes=[pltpu.VMEM((count * share, LANES), f32)],
        compiler_params=params(),
        name="result",
    )(turn, select, *blocks)


def solution(mesh):
    in_specs = (
        P(None, ("groups", "beam"), "tile", None),
        P(None, "beam"),
        P(("groups", "tile"), None),
    )
    out_specs = P(("groups", "tile"), "beam", None)
    return jax.shard_map(
        per_device, mesh=mesh, in_specs=in_specs, out_specs=out_specs, check_vma=False
    )
```

```python
import functools
import math

import jax
import jax.numpy as jnp
from jax import lax
from jax.experimental import pallas as pl
from jax.experimental.pallas import tpu as pltpu
from jax.sharding import PartitionSpec as P

IF = 4
BIN = 2
CAP = 2
PER_LIST = 2 * CAP
LANES = 128
GROUP = 8
CHUNKS = 1
ROWS = 8

LISTS_ORDER = (0, 1, 3, 2)
RESULTS_ORDER = (0, 1, 3, 2)


def orders(n_tile):
    if n_tile == 4:
        return LISTS_ORDER, RESULTS_ORDER
    return tuple(range(n_tile)), tuple(range(n_tile))


two_pi = 2.0 * math.pi
f32 = jnp.float32
bf16 = jnp.bfloat16
i32 = jnp.int32


def iota(shape, dim):
    return lax.broadcasted_iota(i32, shape, dim)


def series(square, last):
    total = jnp.full_like(square, (-1.0) ** (last // 2) / math.factorial(last))
    for n in range(last - 2, -1, -2):
        total = total * square + (-1.0) ** (n // 2) / math.factorial(n)
    return total


def cos_sin(turn):
    x = (turn - jnp.floor(turn + 0.5)) * two_pi
    square = x * x
    return series(square, 18), series(square, 19) * x


def angle_of(index, window):
    half = window // 2
    return (two_pi / window) * (jnp.bitwise_and(index + half, window - 1) - half).astype(f32)


def cosine_of(index, window):
    angle = angle_of(index, window)
    return series(angle * angle, 18)


def bit_reversed(number, count):
    bits = count.bit_length() - 1
    return sum(((number >> b) & 1) << (bits - 1 - b) for b in range(bits))


def window_start(row, window, field_rows):
    start = jnp.right_shift(row, 2) - window // 2
    start = jnp.where(start < 0, start + field_rows, start)
    tile = jnp.right_shift(start, window.bit_length() - 1)
    return tile, jnp.bitwise_and(start, window - 1)


def times_i(pairs):
    return pltpu.roll(pairs, LANES // 2, pairs.ndim - 1)


def spectra_kernel(
    sizes, probes_hbm, smatrix_hbm, table_hbm, spectra, row_table, turn, select, beam_turns, *scratch
):
    window, kept, n_tile, n_beam = sizes
    share = kept // n_beam
    me_beam = lax.axis_index("beam")
    me_tile = lax.axis_index("tile")
    column_table, smatrix, probes, beam_table, sems = scratch
    planes = smatrix.shape[1] // CHUNKS
    chunks = [pl.ds(i * planes, planes) for i in range(CHUNKS)]
    copies = [
        pltpu.make_async_copy(smatrix_hbm.at[:, chunk], smatrix.at[:, chunk], sems.at[i])
        for i, chunk in enumerate(chunks)
    ]
    for copy in copies:
        copy.start()
    listed = pltpu.make_async_copy(probes_hbm, probes, sems.at[CHUNKS])
    listed.start()
    tabled = pltpu.make_async_copy(table_hbm, beam_table, sems.at[CHUNKS + 1])
    tabled.start()

    shape = (2 * window, 2 * kept)
    x, part_in = iota(shape, 0) % window, iota(shape, 0) // window
    lane = iota(shape, 1)
    v, part_out = lane % kept - kept // 2, lane // kept
    index = x * v + (window // 4) * (part_out - part_in)
    column_table[...] = cosine_of(index, window).astype(bf16)

    shape = (2 * kept, 2 * window)
    line, turned = iota(shape, 0) % kept, iota(shape, 0) // kept
    r, part_in = iota(shape, 1) % window, iota(shape, 1) // window
    block = line // share
    owner = jnp.zeros_like(block)
    for pos in range(n_beam):
        owner = jnp.where(block == pos, jnp.bitwise_xor(me_beam, bit_reversed(pos, n_beam)), owner)
    u = owner * share + line % share - kept // 2
    index = u * r + (window // 4) * (turned - part_in)
    row_table[...] = cosine_of(index, window).astype(bf16)

    u = iota((share, LANES), 0) + me_beam * share - kept // 2
    lane = iota((share, LANES), 1)
    v = lane % kept - kept // 2
    tabled.wait()
    beams, wide = beam_table.shape[1], beam_turns.shape[1]
    spread = (iota((beams, wide), 1) // ROWS == iota((beams, wide), 0)).astype(f32)
    wave_numbers = beam_table[...]
    scale = jnp.where(iota(wave_numbers.shape, 0) < 2, 1.0 / (window * IF), 1.0 / two_pi)
    beam_turns[...] = jnp.dot(
        wave_numbers * scale, spread, precision=lax.Precision.HIGHEST, preferred_element_type=f32
    )

    listed.wait()
    shape = (select.shape[0], select.shape[1])
    window_of, slot_of = iota(shape, 0) // share, iota(shape, 1) // share
    wanted = (slot_of == -1, slot_of == -1)
    tiles = []
    for j in range(probes.shape[1]):
        tile, offset = window_start(probes[0, j], window, window * n_tile)
        following = jnp.where(tile == n_tile - 1, 0, tile + 1)
        rank = sum([(t == tile).astype(i32) for t in tiles], i32(0))
        tiles.append(tile)
        spots = [
            (jnp.where(t < me_tile, t + n_tile, t) - me_tile) * PER_LIST + base + rank
            for t, base in ((tile, 0), (following, CAP))
        ]
        wanted = [w | ((window_of == j) & (slot_of == spot)) for w, spot in zip(wanted, spots)]
        shift = jnp.right_shift(probes[1, j], 2) - window // 2
        angle = angle_of(u * offset + v * shift, window)
        square = angle * angle
        turn[0, j * share : (j + 1) * share, :] = series(square, 18)
        turn[1, j * share : (j + 1) * share, :] = series(square, 19) * jnp.where(lane < kept, -angle, angle)
    same_line = iota(shape, 0) % share == iota(shape, 1) % share
    select[...] = jnp.where((wanted[0] | wanted[1]) & same_line, 1.0, 0.0).astype(bf16)

    for i, (copy, chunk) in enumerate(zip(copies, chunks)):
        copy.wait()
        flat = jnp.concatenate([smatrix[c, chunk].reshape(planes * window, window) for c in range(2)], axis=1)
        product = jnp.dot(flat, column_table[...], preferred_element_type=f32)
        product = product.reshape(planes, window // ROWS, ROWS, 2 * kept)
        for t in range(window // ROWS):
            rows = slice(i * planes * ROWS, (i + 1) * planes * ROWS)
            spectra[t, rows, :] = product[:, t].reshape(planes * ROWS, 2 * kept).astype(bf16)


def chosen(lists, me_tile, window, n_tile):
    shape = (len(lists) * PER_LIST, lists[0].shape[1])
    slot, item = iota(shape, 0), iota(shape, 1)
    rows = jnp.zeros(shape, i32)
    columns = jnp.zeros(shape, i32)
    for n, probes in enumerate(lists):
        here = slot // PER_LIST == n
        rows = jnp.where(here, probes[0:1, :], rows)
        columns = jnp.where(here, probes[1:2, :], columns)
    tile, _ = window_start(rows, window, window * n_tile)
    before = jnp.where(me_tile == 0, n_tile - 1, me_tile - 1)
    match = tile == jnp.where(slot % PER_LIST < CAP, me_tile, before)
    sign = jnp.where(slot % CAP == 0, 1, -1)
    nothing = float(1 << 23)
    found = []
    for values, limit in ((rows, window * n_tile * IF), (columns, window * IF)):
        keys = (sign * (item * limit + values)).astype(f32)
        key = jnp.abs(jnp.min(jnp.where(match, keys, nothing), axis=1, keepdims=True))
        found.append(jnp.bitwise_and(key.astype(i32), limit - 1))
    return found


def coefficients_kernel(sizes, *refs):
    window, kept, n_tile, n_beam = sizes
    lists, (beam_turns, row_table, spectra, keep, send, later, later_offsets, coeff, waves) = refs[:-9], refs[-9:]
    slots = len(lists) * PER_LIST
    wide = beam_turns.shape[1]
    now = keep.shape[1] * PER_LIST
    me_tile = lax.axis_index("tile")
    row_v, column_v = chosen(lists, me_tile, window, n_tile)
    offsets = jnp.bitwise_and(jnp.right_shift(row_v, 2) - window // 2, window - 1)
    offsets = jnp.broadcast_to(offsets, (slots, LANES))
    later_offsets[...] = offsets[now:]
    alpha_re, alpha_im = cos_sin(
        beam_turns[2:3, :] + (beam_turns[0:1, :] * row_v.astype(f32) + beam_turns[1:2, :] * column_v.astype(f32))
    )
    pair = iota((2 * ROWS, wide), 0)
    own_row = iota((2 * ROWS, wide), 1) % ROWS == pair % ROWS
    for c, alpha in enumerate((alpha_re, -alpha_im)):
        for p in range(0, slots, 2):
            lines = jnp.where(pair < ROWS, alpha[p : p + 1, :], alpha[p + 1 : p + 2, :])
            lines = jnp.where(own_row, lines, 0.0).astype(bf16)
            if p < now:
                coeff[p // GROUP, c, p % GROUP // 2] = lines
            else:
                later[(p - now) // GROUP, c, (p - now) % GROUP // 2] = lines
    make_parts(sizes, coeff, offsets[:now], row_table, spectra, keep, send, waves)


def parts_kernel(sizes, coeff, offsets, row_table, spectra, keep, send, waves):
    make_parts(sizes, coeff, offsets[...], row_table, spectra, keep, send, waves)


def make_parts(sizes, coeff, offsets, row_table, spectra, keep, send, waves):
    window, kept, n_tile, n_beam = sizes
    share = kept // n_beam
    y_in = iota((2 * ROWS, LANES), 0)
    lane = iota((kept, LANES), 1)
    sign = jnp.where(lane < kept, -1.0, 1.0)
    for group in range(coeff.shape[0]):
        first = group * GROUP
        matrix = coeff[group].reshape(2 * GROUP * ROWS, spectra.shape[1])
        for t in range(0, spectra.shape[0], 2):
            pair = jnp.concatenate([spectra[t], spectra[t + 1]], axis=1)
            made = jnp.dot(matrix, pair, preferred_element_type=f32)
            y = t * ROWS
            for p in range(GROUP):
                offset = offsets[first + p : first + p + 1, :]
                starts_here = p % PER_LIST < CAP
                inside = y_in + y >= offset if starts_here else y_in + y < offset
                for c in range(2):
                    spot = (c * GROUP + p) * ROWS
                    value = made[spot : spot + ROWS, :]
                    value = jnp.concatenate([value[:, :LANES], value[:, LANES:]], axis=0)
                    waves[c, p, y : y + 2 * ROWS, :] = jnp.where(inside, value, 0.0).astype(bf16)
        for p in range(0, GROUP, PER_LIST):
            fields = []
            for q in range(p, p + PER_LIST, 2):
                pair = jnp.concatenate(
                    [waves[:, q + h].reshape(2 * window, LANES) for h in range(2)], axis=1
                )
                both = jnp.dot(row_table[...], pair, preferred_element_type=f32)
                for h in range(2):
                    value = both[:, h * LANES : (h + 1) * LANES]
                    fields.append(value[:kept] + times_i(value[kept:]) * sign)
            k = (first + p) // PER_LIST
            for pos in range(n_beam):
                block = jnp.concatenate([f[pos * share : (pos + 1) * share] for f in fields], axis=0).astype(bf16)
                half = n_beam // 2
                if pos < half:
                    keep[pos, k] = block
                else:
                    send[pos - half, k] = block


def result_kernel(sizes, all_beams, *refs):
    window, kept, n_tile, n_beam = sizes
    turn, select = refs[:2]
    blocks = in_order(refs[2 : 2 + n_tile], orders(n_tile)[1])
    out, intensity = refs[2 + n_tile :]
    height = select.shape[0] // BIN
    shape = (2 * LANES, kept // BIN)
    bins = (iota(shape, 0) % kept // BIN == iota(shape, 1)).astype(f32).astype(bf16)
    arrived = jnp.concatenate([block[...] for block in blocks], axis=0)
    field = jnp.dot(select[...], arrived, preferred_element_type=f32)
    field = field * turn[0] + times_i(field) * turn[1]
    intensity[...] = field * field
    summed = intensity[pl.ds(0, height, stride=BIN), :]
    for b in range(1, BIN):
        summed = summed + intensity[pl.ds(b, height, stride=BIN), :]
    high = summed.astype(bf16)
    low = (summed - high.astype(f32)).astype(bf16)
    binned = jnp.dot(jnp.concatenate([high, low], axis=1), bins, preferred_element_type=f32)
    binned = binned * (1.0 / (BIN * BIN * window * window * all_beams))
    each = height // out.shape[0]
    for j in range(out.shape[0]):
        out[j] = binned[j * each : (j + 1) * each]


VMEM = pl.BlockSpec(memory_space=pltpu.VMEM)
HBM = pl.BlockSpec(memory_space=pltpu.HBM)


def params(mib=16):
    return pltpu.CompilerParams(vmem_limit_bytes=mib * 1024 * 1024)


def swapped(array, axis, by):
    return lax.ppermute(array, axis, [(i, i ^ by) for i in range(lax.axis_size(axis))])


def shifted(arrays, way, order):
    size = lax.axis_size("tile")
    return [
        lax.ppermute(arrays[k], "tile", [(i, (i + way * k) % size) for i in range(size)]) if k else arrays[0]
        for k in order
    ]


def halves(n_tile):
    numbers = list(range(n_tile))[::-1]
    return numbers[: n_tile // 2], numbers[n_tile // 2 :]


def in_order(refs, order):
    return [refs[order.index(k)] for k in range(len(order))]


def per_device(smatrix, beam_table, probes):
    _, beams, window, _ = smatrix.shape
    kept = window // 2
    n_tile = lax.axis_size("tile")
    n_beam = lax.axis_size("beam")
    sizes = (window, kept, n_tile, n_beam)
    share = kept // n_beam
    slots = n_tile * PER_LIST
    count = probes.shape[0]

    probes = probes.T
    lists_order, results_order = orders(n_tile)
    lists = lax.optimization_barrier(shifted([probes] * n_tile, 1, lists_order))
    lists = dict(zip(lists_order, lists))

    spectra, row_table, turn, select, beam_turns = pl.pallas_call(
        functools.partial(spectra_kernel, sizes),
        in_specs=[HBM, HBM, HBM],
        out_specs=[VMEM] * 5,
        out_shape=[
            jax.ShapeDtypeStruct((window // ROWS, beams * ROWS, 2 * kept), bf16),
            jax.ShapeDtypeStruct((2 * kept, 2 * window), bf16),
            jax.ShapeDtypeStruct((2, count * share, LANES), f32),
            jax.ShapeDtypeStruct((count * share, slots * share), bf16),
            jax.ShapeDtypeStruct((3, beams * ROWS), f32),
        ],
        scratch_shapes=[
            pltpu.VMEM((2 * window, 2 * kept), bf16),
            pltpu.VMEM(smatrix.shape, bf16),
            pltpu.SMEM(probes.shape, i32),
            pltpu.VMEM(beam_table.shape, f32),
            pltpu.SemaphoreType.DMA((CHUNKS + 2,)),
        ],
        compiler_params=params(48),
        cost_estimate=pl.CostEstimate(
            flops=2 * beams * window * 4 * window * kept, bytes_accessed=smatrix.size * 3, transcendentals=0
        ),
        name="spectra",
    )(
        pltpu.with_memory_space_constraint(probes, pltpu.HBM),
        pltpu.with_memory_space_constraint(smatrix, pltpu.HBM),
        pltpu.with_memory_space_constraint(beam_table, pltpu.HBM),
    )

    earlier, later = halves(n_tile)

    def parts_call(kernel, numbers, operands, more, scratch, name):
        half = jax.ShapeDtypeStruct((n_beam // 2, len(numbers), PER_LIST * share, LANES), bf16)
        return pl.pallas_call(
            functools.partial(kernel, sizes),
            in_specs=[VMEM] * len(operands),
            out_specs=[VMEM] * (2 + len(more)),
            out_shape=[half, half, *more],
            scratch_shapes=[*scratch, pltpu.VMEM((2, GROUP, window, LANES), bf16)],
            compiler_params=params(),
            cost_estimate=pl.CostEstimate(
                flops=2 * len(numbers) * PER_LIST * 2 * ROWS * beams * window * LANES,
                bytes_accessed=4 * 1024 * 1024,
                transcendentals=0,
            ),
            name=name,
        )(*operands)

    coeff_shape = (len(earlier) * PER_LIST // GROUP, 2, GROUP // 2, 2 * ROWS, beams * ROWS)
    keep, send, coeff, offsets = parts_call(
        coefficients_kernel,
        earlier,
        [lists[n] for n in earlier + later] + [beam_turns, row_table, spectra],
        [
            jax.ShapeDtypeStruct(coeff_shape, bf16),
            jax.ShapeDtypeStruct((len(later) * PER_LIST, LANES), i32),
        ],
        [pltpu.VMEM(coeff_shape, bf16)],
        "coefficients",
    )
    halves_made = [
        (earlier, keep, send),
        (later, *parts_call(parts_kernel, later, [coeff, offsets, row_table, spectra], [], [], "parts")),
    ]

    results = {}
    for numbers, keep, send in halves_made:
        by = 1
        while by < n_beam:
            arrived = swapped(send, "beam", by)
            total = (keep.astype(f32) + arrived.astype(f32)).astype(bf16)
            by *= 2
            middle = total.shape[0] // 2
            keep, send = total[:middle], total[middle:]
        results |= {n: total[0, i] for i, n in enumerate(numbers)}
    blocks = shifted(results, -1, results_order)

    return pl.pallas_call(
        functools.partial(result_kernel, sizes, beams * n_beam),
        in_specs=[VMEM] * (2 + n_tile),
        out_specs=VMEM,
        out_shape=jax.ShapeDtypeStruct((count, share // BIN, kept // BIN), f32),
        scratch_shapes=[pltpu.VMEM((count * share, LANES), f32)],
        compiler_params=params(),
        name="result",
    )(turn, select, *blocks)


def solution(mesh):
    in_specs = (
        P(None, ("groups", "beam"), "tile", None),
        P(None, "beam"),
        P(("groups", "tile"), None),
    )
    out_specs = P(("groups", "tile"), "beam", None)
    return jax.shard_map(
        per_device, mesh=mesh, in_specs=in_specs, out_specs=out_specs, check_vma=False
    )
```

```python
import functools
import math

import jax
import jax.numpy as jnp
from jax import lax
from jax.experimental import pallas as pl
from jax.experimental.pallas import tpu as pltpu
from jax.sharding import PartitionSpec as P

IF = 4
BIN = 2
CAP = 2
PER_LIST = 2 * CAP
LANES = 128
GROUP = 8
CHUNKS = 2
ROWS = 8

LISTS_ORDER = (0, 1, 3, 2)
RESULTS_ORDER = (0, 1, 3, 2)


def orders(n_tile):
    if n_tile == 4:
        return LISTS_ORDER, RESULTS_ORDER
    return tuple(range(n_tile)), tuple(range(n_tile))


two_pi = 2.0 * math.pi
f32 = jnp.float32
bf16 = jnp.bfloat16
i32 = jnp.int32


def iota(shape, dim):
    return lax.broadcasted_iota(i32, shape, dim)


def series(square, last):
    total = jnp.full_like(square, (-1.0) ** (last // 2) / math.factorial(last))
    for n in range(last - 2, -1, -2):
        total = total * square + (-1.0) ** (n // 2) / math.factorial(n)
    return total


def cos_sin(turn):
    x = (turn - jnp.floor(turn + 0.5)) * two_pi
    square = x * x
    return series(square, 18), series(square, 19) * x


def angle_of(index, window):
    half = window // 2
    return (two_pi / window) * (jnp.bitwise_and(index + half, window - 1) - half).astype(f32)


def cosine_of(index, window):
    angle = angle_of(index, window)
    return series(angle * angle, 18)


def bit_reversed(number, count):
    bits = count.bit_length() - 1
    return sum(((number >> b) & 1) << (bits - 1 - b) for b in range(bits))


def window_start(row, window, field_rows):
    start = jnp.right_shift(row, 2) - window // 2
    start = jnp.where(start < 0, start + field_rows, start)
    tile = jnp.right_shift(start, window.bit_length() - 1)
    return tile, jnp.bitwise_and(start, window - 1)


def times_i(pairs):
    return pltpu.roll(pairs, LANES // 2, pairs.ndim - 1)


def spectra_kernel(
    sizes, smatrix_hbm, table_hbm, spectra, row_table, beam_turns, *scratch
):
    window, kept, n_tile, n_beam = sizes
    share = kept // n_beam
    me_beam = lax.axis_index("beam")
    column_table, smatrix, beam_table, sems = scratch
    planes = smatrix.shape[1] // CHUNKS

    def arrival(i):
        chunk = pl.ds(i * planes, planes)
        return pltpu.make_async_copy(smatrix_hbm.at[:, chunk], smatrix.at[:, chunk], sems.at[i])

    for i in range(CHUNKS):
        arrival(i).start()
    tabled = pltpu.make_async_copy(table_hbm, beam_table, sems.at[CHUNKS])
    tabled.start()

    shape = (2 * window, 2 * kept)
    x, part_in = iota(shape, 0) % window, iota(shape, 0) // window
    lane = iota(shape, 1)
    v, part_out = lane % kept - kept // 2, lane // kept
    index = x * v + (window // 4) * (part_out - part_in)
    column_table[...] = cosine_of(index, window).astype(bf16)

    def transform(i, carry):
        arrival(i).wait()
        chunk = pl.ds(i * planes, planes)
        flat = jnp.concatenate([smatrix[c, chunk].reshape(planes * window, window) for c in range(2)], axis=1)
        product = jnp.dot(flat, column_table[...], preferred_element_type=f32)
        product = product.reshape(planes, window // ROWS, ROWS, 2 * kept)
        rows = pl.ds(pl.multiple_of(i * planes * ROWS, planes * ROWS), planes * ROWS)
        for t in range(window // ROWS):
            spectra[t, rows, :] = product[:, t].reshape(planes * ROWS, 2 * kept).astype(bf16)
        return carry

    lax.fori_loop(0, CHUNKS, transform, 0)

    shape = (2 * kept, 2 * window)
    line, turned = iota(shape, 0) % kept, iota(shape, 0) // kept
    r, part_in = iota(shape, 1) % window, iota(shape, 1) // window
    block = line // share
    owner = jnp.zeros_like(block)
    for pos in range(n_beam):
        owner = jnp.where(block == pos, jnp.bitwise_xor(me_beam, bit_reversed(pos, n_beam)), owner)
    u = owner * share + line % share - kept // 2
    index = u * r + (window // 4) * (turned - part_in)
    row_table[...] = cosine_of(index, window).astype(bf16)

    tabled.wait()
    beams, wide = beam_table.shape[1], beam_turns.shape[1]
    spread = (iota((beams, wide), 1) // ROWS == iota((beams, wide), 0)).astype(f32)
    wave_numbers = beam_table[...]
    scale = jnp.where(iota(wave_numbers.shape, 0) < 2, 1.0 / (window * IF), 1.0 / two_pi)
    beam_turns[...] = jnp.dot(
        wave_numbers * scale, spread, precision=lax.Precision.HIGHEST, preferred_element_type=f32
    )


def homing_kernel(sizes, probes, turn, select):
    window, kept, n_tile, n_beam = sizes
    share = kept // n_beam
    me_beam = lax.axis_index("beam")
    me_tile = lax.axis_index("tile")
    u = iota((share, LANES), 0) + me_beam * share - kept // 2
    lane = iota((share, LANES), 1)
    v = lane % kept - kept // 2
    shape = (select.shape[0], select.shape[1])
    window_of, slot_of = iota(shape, 0) // share, iota(shape, 1) // share
    wanted = (slot_of == -1, slot_of == -1)
    tiles = []
    for j in range(probes.shape[1]):
        tile, offset = window_start(probes[0, j], window, window * n_tile)
        following = jnp.where(tile == n_tile - 1, 0, tile + 1)
        rank = sum([(t == tile).astype(i32) for t in tiles], i32(0))
        tiles.append(tile)
        spots = [
            (jnp.where(t < me_tile, t + n_tile, t) - me_tile) * PER_LIST + base + rank
            for t, base in ((tile, 0), (following, CAP))
        ]
        wanted = [w | ((window_of == j) & (slot_of == spot)) for w, spot in zip(wanted, spots)]
        shift = jnp.right_shift(probes[1, j], 2) - window // 2
        angle = angle_of(u * offset + v * shift, window)
        square = angle * angle
        turn[0, j * share : (j + 1) * share, :] = series(square, 18)
        turn[1, j * share : (j + 1) * share, :] = series(square, 19) * jnp.where(lane < kept, -angle, angle)
    same_line = iota(shape, 0) % share == iota(shape, 1) % share
    select[...] = jnp.where((wanted[0] | wanted[1]) & same_line, 1.0, 0.0).astype(bf16)


def chosen(lists, me_tile, window, n_tile):
    shape = (len(lists) * PER_LIST, lists[0].shape[1])
    slot, item = iota(shape, 0), iota(shape, 1)
    rows = jnp.zeros(shape, i32)
    columns = jnp.zeros(shape, i32)
    for n, probes in enumerate(lists):
        here = slot // PER_LIST == n
        rows = jnp.where(here, probes[0:1, :], rows)
        columns = jnp.where(here, probes[1:2, :], columns)
    tile, _ = window_start(rows, window, window * n_tile)
    before = jnp.where(me_tile == 0, n_tile - 1, me_tile - 1)
    match = tile == jnp.where(slot % PER_LIST < CAP, me_tile, before)
    sign = jnp.where(slot % CAP == 0, 1, -1)
    nothing = float(1 << 23)
    found = []
    for values, limit in ((rows, window * n_tile * IF), (columns, window * IF)):
        keys = (sign * (item * limit + values)).astype(f32)
        key = jnp.abs(jnp.min(jnp.where(match, keys, nothing), axis=1, keepdims=True))
        found.append(jnp.bitwise_and(key.astype(i32), limit - 1))
    return found


def coefficients_kernel(sizes, *refs):
    window, kept, n_tile, n_beam = sizes
    lists, (beam_turns, row_table, spectra, keep, send, later, later_offsets, coeff, waves) = refs[:-9], refs[-9:]
    slots = len(lists) * PER_LIST
    wide = beam_turns.shape[1]
    now = keep.shape[1] * PER_LIST
    me_tile = lax.axis_index("tile")
    row_v, column_v = chosen(lists, me_tile, window, n_tile)
    offsets = jnp.bitwise_and(jnp.right_shift(row_v, 2) - window // 2, window - 1)
    offsets = jnp.broadcast_to(offsets, (slots, LANES))
    later_offsets[...] = offsets[now:]
    alpha_re, alpha_im = cos_sin(
        beam_turns[2:3, :] + (beam_turns[0:1, :] * row_v.astype(f32) + beam_turns[1:2, :] * column_v.astype(f32))
    )
    pair = iota((2 * ROWS, wide), 0)
    own_row = iota((2 * ROWS, wide), 1) % ROWS == pair % ROWS
    for c, alpha in enumerate((alpha_re, -alpha_im)):
        for p in range(0, slots, 2):
            lines = jnp.where(pair < ROWS, alpha[p : p + 1, :], alpha[p + 1 : p + 2, :])
            lines = jnp.where(own_row, lines, 0.0).astype(bf16)
            if p < now:
                coeff[p // GROUP, c, p % GROUP // 2] = lines
            else:
                later[(p - now) // GROUP, c, (p - now) % GROUP // 2] = lines
    make_parts(sizes, coeff, offsets[:now], row_table, spectra, keep, send, waves)


def parts_kernel(sizes, coeff, offsets, row_table, spectra, keep, send, waves):
    make_parts(sizes, coeff, offsets[...], row_table, spectra, keep, send, waves)


def make_parts(sizes, coeff, offsets, row_table, spectra, keep, send, waves):
    window, kept, n_tile, n_beam = sizes
    share = kept // n_beam
    y_in = iota((2 * ROWS, LANES), 0)
    lane = iota((kept, LANES), 1)
    sign = jnp.where(lane < kept, -1.0, 1.0)
    for group in range(coeff.shape[0]):
        first = group * GROUP
        matrix = coeff[group].reshape(2 * GROUP * ROWS, spectra.shape[1])
        for t in range(0, spectra.shape[0], 2):
            pair = jnp.concatenate([spectra[t], spectra[t + 1]], axis=1)
            made = jnp.dot(matrix, pair, preferred_element_type=f32)
            y = t * ROWS
            for p in range(GROUP):
                offset = offsets[first + p : first + p + 1, :]
                starts_here = p % PER_LIST < CAP
                inside = y_in + y >= offset if starts_here else y_in + y < offset
                for c in range(2):
                    spot = (c * GROUP + p) * ROWS
                    value = made[spot : spot + ROWS, :]
                    value = jnp.concatenate([value[:, :LANES], value[:, LANES:]], axis=0)
                    waves[c, p, y : y + 2 * ROWS, :] = jnp.where(inside, value, 0.0).astype(bf16)
        for p in range(0, GROUP, PER_LIST):
            fields = []
            for q in range(p, p + PER_LIST, 2):
                pair = jnp.concatenate(
                    [waves[:, q + h].reshape(2 * window, LANES) for h in range(2)], axis=1
                )
                both = jnp.dot(row_table[...], pair, preferred_element_type=f32)
                for h in range(2):
                    value = both[:, h * LANES : (h + 1) * LANES]
                    fields.append(value[:kept] + times_i(value[kept:]) * sign)
            k = (first + p) // PER_LIST
            for pos in range(n_beam):
                block = jnp.concatenate([f[pos * share : (pos + 1) * share] for f in fields], axis=0).astype(bf16)
                half = n_beam // 2
                if pos < half:
                    keep[pos, k] = block
                else:
                    send[pos - half, k] = block


def result_kernel(sizes, all_beams, *refs):
    window, kept, n_tile, n_beam = sizes
    turn, select = refs[:2]
    blocks = in_order(refs[2 : 2 + n_tile], orders(n_tile)[1])
    out, intensity = refs[2 + n_tile :]
    height = select.shape[0] // BIN
    shape = (2 * LANES, kept // BIN)
    bins = (iota(shape, 0) % kept // BIN == iota(shape, 1)).astype(f32).astype(bf16)
    arrived = jnp.concatenate([block[...] for block in blocks], axis=0)
    field = jnp.dot(select[...], arrived, preferred_element_type=f32)
    field = field * turn[0] + times_i(field) * turn[1]
    intensity[...] = field * field
    summed = intensity[pl.ds(0, height, stride=BIN), :]
    for b in range(1, BIN):
        summed = summed + intensity[pl.ds(b, height, stride=BIN), :]
    high = summed.astype(bf16)
    low = (summed - high.astype(f32)).astype(bf16)
    binned = jnp.dot(jnp.concatenate([high, low], axis=1), bins, preferred_element_type=f32)
    binned = binned * (1.0 / (BIN * BIN * window * window * all_beams))
    each = height // out.shape[0]
    for j in range(out.shape[0]):
        out[j] = binned[j * each : (j + 1) * each]


VMEM = pl.BlockSpec(memory_space=pltpu.VMEM)
HBM = pl.BlockSpec(memory_space=pltpu.HBM)
SMEM = pl.BlockSpec(memory_space=pltpu.SMEM)


def params(mib=16):
    return pltpu.CompilerParams(vmem_limit_bytes=mib * 1024 * 1024)


def swapped(array, axis, by):
    return lax.ppermute(array, axis, [(i, i ^ by) for i in range(lax.axis_size(axis))])


def shifted(arrays, way, order):
    size = lax.axis_size("tile")
    return [
        lax.ppermute(arrays[k], "tile", [(i, (i + way * k) % size) for i in range(size)]) if k else arrays[0]
        for k in order
    ]


def halves(n_tile):
    numbers = list(range(n_tile))[::-1]
    return numbers[: n_tile // 2], numbers[n_tile // 2 :]


def in_order(refs, order):
    return [refs[order.index(k)] for k in range(len(order))]


def per_device(smatrix, beam_table, probes):
    _, beams, window, _ = smatrix.shape
    kept = window // 2
    n_tile = lax.axis_size("tile")
    n_beam = lax.axis_size("beam")
    sizes = (window, kept, n_tile, n_beam)
    share = kept // n_beam
    slots = n_tile * PER_LIST
    count = probes.shape[0]

    probes = probes.T
    lists_order, results_order = orders(n_tile)
    lists = lax.optimization_barrier(shifted([probes] * n_tile, 1, lists_order))
    lists = dict(zip(lists_order, lists))

    turn, select = pl.pallas_call(
        functools.partial(homing_kernel, sizes),
        in_specs=[SMEM],
        out_specs=[VMEM] * 2,
        out_shape=[
            jax.ShapeDtypeStruct((2, count * share, LANES), f32),
            jax.ShapeDtypeStruct((count * share, slots * share), bf16),
        ],
        compiler_params=params(),
        cost_estimate=pl.CostEstimate(flops=1 << 28, bytes_accessed=1 << 20, transcendentals=0),
        name="homing",
    )(probes)
    spectra, row_table, beam_turns = pl.pallas_call(
        functools.partial(spectra_kernel, sizes),
        in_specs=[HBM, HBM],
        out_specs=[VMEM] * 3,
        out_shape=[
            jax.ShapeDtypeStruct((window // ROWS, beams * ROWS, 2 * kept), bf16),
            jax.ShapeDtypeStruct((2 * kept, 2 * window), bf16),
            jax.ShapeDtypeStruct((3, beams * ROWS), f32),
        ],
        scratch_shapes=[
            pltpu.VMEM((2 * window, 2 * kept), bf16),
            pltpu.VMEM(smatrix.shape, bf16),
            pltpu.VMEM(beam_table.shape, f32),
            pltpu.SemaphoreType.DMA((CHUNKS + 1,)),
        ],
        compiler_params=params(48),
        cost_estimate=pl.CostEstimate(
            flops=2 * beams * window * 4 * window * kept, bytes_accessed=smatrix.size * 3, transcendentals=0
        ),
        name="spectra",
    )(
        pltpu.with_memory_space_constraint(smatrix, pltpu.HBM),
        pltpu.with_memory_space_constraint(beam_table, pltpu.HBM),
    )

    earlier, later = halves(n_tile)

    def parts_call(kernel, numbers, operands, more, scratch, name):
        half = jax.ShapeDtypeStruct((n_beam // 2, len(numbers), PER_LIST * share, LANES), bf16)
        return pl.pallas_call(
            functools.partial(kernel, sizes),
            in_specs=[VMEM] * len(operands),
            out_specs=[VMEM] * (2 + len(more)),
            out_shape=[half, half, *more],
            scratch_shapes=[*scratch, pltpu.VMEM((2, GROUP, window, LANES), bf16)],
            compiler_params=params(),
            cost_estimate=pl.CostEstimate(
                flops=2 * len(numbers) * PER_LIST * 2 * ROWS * beams * window * LANES,
                bytes_accessed=4 * 1024 * 1024,
                transcendentals=0,
            ),
            name=name,
        )(*operands)

    coeff_shape = (len(earlier) * PER_LIST // GROUP, 2, GROUP // 2, 2 * ROWS, beams * ROWS)
    keep, send, coeff, offsets = parts_call(
        coefficients_kernel,
        earlier,
        [lists[n] for n in earlier + later] + [beam_turns, row_table, spectra],
        [
            jax.ShapeDtypeStruct(coeff_shape, bf16),
            jax.ShapeDtypeStruct((len(later) * PER_LIST, LANES), i32),
        ],
        [pltpu.VMEM(coeff_shape, bf16)],
        "coefficients",
    )
    halves_made = [
        (earlier, keep, send),
        (later, *parts_call(parts_kernel, later, [coeff, offsets, row_table, spectra], [], [], "parts")),
    ]

    results = {}
    for numbers, keep, send in halves_made:
        by = 1
        while by < n_beam:
            arrived = swapped(send, "beam", by)
            total = (keep.astype(f32) + arrived.astype(f32)).astype(bf16)
            by *= 2
            middle = total.shape[0] // 2
            keep, send = total[:middle], total[middle:]
        results |= {n: total[0, i] for i, n in enumerate(numbers)}
    blocks = shifted(results, -1, results_order)

    return pl.pallas_call(
        functools.partial(result_kernel, sizes, beams * n_beam),
        in_specs=[VMEM] * (2 + n_tile),
        out_specs=VMEM,
        out_shape=jax.ShapeDtypeStruct((count, share // BIN, kept // BIN), f32),
        scratch_shapes=[pltpu.VMEM((count * share, LANES), f32)],
        compiler_params=params(),
        name="result",
    )(turn, select, *blocks)


def solution(mesh):
    in_specs = (
        P(None, ("groups", "beam"), "tile", None),
        P(None, "beam"),
        P(("groups", "tile"), None),
    )
    out_specs = P(("groups", "tile"), "beam", None)
    return jax.shard_map(
        per_device, mesh=mesh, in_specs=in_specs, out_specs=out_specs, check_vma=False
    )
```

```python
import functools
import math

import jax
import jax.numpy as jnp
from jax import lax
from jax.experimental import pallas as pl
from jax.experimental.pallas import tpu as pltpu
from jax.sharding import PartitionSpec as P

IF = 4
BIN = 2
CAP = 2
PER_LIST = 2 * CAP
LANES = 128
GROUP = 8
CHUNKS = 2
ROWS = 8

LISTS_ORDER = (0, 1, 3, 2)
RESULTS_ORDER = (0, 1, 3, 2)


def orders(n_tile):
    if n_tile == 4:
        return LISTS_ORDER, RESULTS_ORDER
    return tuple(range(n_tile)), tuple(range(n_tile))


two_pi = 2.0 * math.pi
f32 = jnp.float32
bf16 = jnp.bfloat16
i32 = jnp.int32


def iota(shape, dim):
    return lax.broadcasted_iota(i32, shape, dim)


def series(square, last):
    total = jnp.full_like(square, (-1.0) ** (last // 2) / math.factorial(last))
    for n in range(last - 2, -1, -2):
        total = total * square + (-1.0) ** (n // 2) / math.factorial(n)
    return total


def cos_sin(turn):
    x = (turn - jnp.floor(turn + 0.5)) * two_pi
    square = x * x
    return series(square, 18), series(square, 19) * x


def angle_of(index, window):
    half = window // 2
    return (two_pi / window) * (jnp.bitwise_and(index + half, window - 1) - half).astype(f32)


def cosine_of(index, window):
    angle = angle_of(index, window)
    return series(angle * angle, 18)


def bit_reversed(number, count):
    bits = count.bit_length() - 1
    return sum(((number >> b) & 1) << (bits - 1 - b) for b in range(bits))


def window_start(row, window, field_rows):
    start = jnp.right_shift(row, 2) - window // 2
    start = jnp.where(start < 0, start + field_rows, start)
    tile = jnp.right_shift(start, window.bit_length() - 1)
    return tile, jnp.bitwise_and(start, window - 1)


def times_i(pairs):
    return pltpu.roll(pairs, LANES // 2, pairs.ndim - 1)


def spectra_kernel(
    sizes, smatrix_hbm, table_hbm, spectra, row_table, beam_turns, *scratch
):
    window, kept, n_tile, n_beam = sizes
    share = kept // n_beam
    me_beam = lax.axis_index("beam")
    column_table, smatrix, beam_table, sems = scratch
    planes = smatrix.shape[1] // CHUNKS

    def arrival(i):
        chunk = pl.ds(i * planes, planes)
        return pltpu.make_async_copy(smatrix_hbm.at[:, chunk], smatrix.at[:, chunk], sems.at[i])

    for i in range(CHUNKS):
        arrival(i).start()
    tabled = pltpu.make_async_copy(table_hbm, beam_table, sems.at[CHUNKS])
    tabled.start()

    shape = (2 * window, 2 * kept)
    x, part_in = iota(shape, 0) % window, iota(shape, 0) // window
    lane = iota(shape, 1)
    v, part_out = lane % kept - kept // 2, lane // kept
    index = x * v + (window // 4) * (part_out - part_in)
    column_table[...] = cosine_of(index, window).astype(bf16)

    shape = (2 * kept, 2 * window)
    line, turned = iota(shape, 0) % kept, iota(shape, 0) // kept
    r, part_in = iota(shape, 1) % window, iota(shape, 1) // window
    block = line // share
    owner = jnp.zeros_like(block)
    for pos in range(n_beam):
        owner = jnp.where(block == pos, jnp.bitwise_xor(me_beam, bit_reversed(pos, n_beam)), owner)
    u = owner * share + line % share - kept // 2
    index = u * r + (window // 4) * (turned - part_in)
    row_table[...] = cosine_of(index, window).astype(bf16)

    def transform(i, carry):
        arrival(i).wait()
        chunk = pl.ds(i * planes, planes)
        flat = jnp.concatenate([smatrix[c, chunk].reshape(planes * window, window) for c in range(2)], axis=1)
        product = jnp.dot(flat, column_table[...], preferred_element_type=f32)
        product = product.reshape(planes, window // ROWS, ROWS, 2 * kept)
        rows = pl.ds(pl.multiple_of(i * planes * ROWS, planes * ROWS), planes * ROWS)
        for t in range(window // ROWS):
            spectra[t, rows, :] = product[:, t].reshape(planes * ROWS, 2 * kept).astype(bf16)
        return carry

    lax.fori_loop(0, CHUNKS, transform, 0)

    tabled.wait()
    beams, wide = beam_table.shape[1], beam_turns.shape[1]
    spread = (iota((beams, wide), 1) // ROWS == iota((beams, wide), 0)).astype(f32).astype(bf16)
    left = beam_table[...]
    left = left * jnp.where(iota(left.shape, 0) < 2, 1.0 / (window * IF), 1.0 / two_pi)
    pieces = []
    for _ in range(3):
        piece = left.astype(bf16)
        left = left - piece.astype(f32)
        pieces.append(jnp.dot(piece, spread, preferred_element_type=f32))
    beam_turns[...] = pieces[0] + (pieces[1] + pieces[2])


def homing_kernel(sizes, probes, turn, select):
    window, kept, n_tile, n_beam = sizes
    share = kept // n_beam
    me_beam = lax.axis_index("beam")
    me_tile = lax.axis_index("tile")
    u = iota((share, LANES), 0) + me_beam * share - kept // 2
    lane = iota((share, LANES), 1)
    v = lane % kept - kept // 2
    shape = (select.shape[0], select.shape[1])
    window_of, slot_of = iota(shape, 0) // share, iota(shape, 1) // share
    wanted = (slot_of == -1, slot_of == -1)
    tiles = []
    for j in range(probes.shape[1]):
        tile, offset = window_start(probes[0, j], window, window * n_tile)
        following = jnp.where(tile == n_tile - 1, 0, tile + 1)
        rank = sum([(t == tile).astype(i32) for t in tiles], i32(0))
        tiles.append(tile)
        spots = [
            (jnp.where(t < me_tile, t + n_tile, t) - me_tile) * PER_LIST + base + rank
            for t, base in ((tile, 0), (following, CAP))
        ]
        wanted = [w | ((window_of == j) & (slot_of == spot)) for w, spot in zip(wanted, spots)]
        shift = jnp.right_shift(probes[1, j], 2) - window // 2
        angle = angle_of(u * offset + v * shift, window)
        square = angle * angle
        turn[0, j * share : (j + 1) * share, :] = series(square, 18)
        turn[1, j * share : (j + 1) * share, :] = series(square, 19) * jnp.where(lane < kept, -angle, angle)
    same_line = iota(shape, 0) % share == iota(shape, 1) % share
    select[...] = jnp.where((wanted[0] | wanted[1]) & same_line, 1.0, 0.0).astype(bf16)


def chosen(lists, me_tile, window, n_tile):
    shape = (len(lists) * PER_LIST, lists[0].shape[1])
    slot, item = iota(shape, 0), iota(shape, 1)
    rows = jnp.zeros(shape, i32)
    columns = jnp.zeros(shape, i32)
    for n, probes in enumerate(lists):
        here = slot // PER_LIST == n
        rows = jnp.where(here, probes[0:1, :], rows)
        columns = jnp.where(here, probes[1:2, :], columns)
    tile, _ = window_start(rows, window, window * n_tile)
    before = jnp.where(me_tile == 0, n_tile - 1, me_tile - 1)
    match = tile == jnp.where(slot % PER_LIST < CAP, me_tile, before)
    sign = jnp.where(slot % CAP == 0, 1, -1)
    nothing = float(1 << 23)
    found = []
    for values, limit in ((rows, window * n_tile * IF), (columns, window * IF)):
        keys = (sign * (item * limit + values)).astype(f32)
        key = jnp.abs(jnp.min(jnp.where(match, keys, nothing), axis=1, keepdims=True))
        found.append(jnp.bitwise_and(key.astype(i32), limit - 1))
    return found


def coefficients_kernel(sizes, *refs):
    window, kept, n_tile, n_beam = sizes
    lists, (beam_turns, row_table, spectra, keep, send, later, later_offsets, coeff, waves) = refs[:-9], refs[-9:]
    slots = len(lists) * PER_LIST
    wide = beam_turns.shape[1]
    now = keep.shape[1] * PER_LIST
    me_tile = lax.axis_index("tile")
    row_v, column_v = chosen(lists, me_tile, window, n_tile)
    offsets = jnp.bitwise_and(jnp.right_shift(row_v, 2) - window // 2, window - 1)
    offsets = jnp.broadcast_to(offsets, (slots, LANES))
    later_offsets[...] = offsets[now:]
    alpha_re, alpha_im = cos_sin(
        beam_turns[2:3, :] + (beam_turns[0:1, :] * row_v.astype(f32) + beam_turns[1:2, :] * column_v.astype(f32))
    )
    pair = iota((2 * ROWS, wide), 0)
    own_row = iota((2 * ROWS, wide), 1) % ROWS == pair % ROWS
    for c, alpha in enumerate((alpha_re, -alpha_im)):
        for p in range(0, slots, 2):
            lines = jnp.where(pair < ROWS, alpha[p : p + 1, :], alpha[p + 1 : p + 2, :])
            lines = jnp.where(own_row, lines, 0.0).astype(bf16)
            if p < now:
                coeff[p // GROUP, c, p % GROUP // 2] = lines
            else:
                later[(p - now) // GROUP, c, (p - now) % GROUP // 2] = lines
    make_parts(sizes, coeff, offsets[:now], row_table, spectra, keep, send, waves)


def parts_kernel(sizes, coeff, offsets, row_table, spectra, keep, send, waves):
    make_parts(sizes, coeff, offsets[...], row_table, spectra, keep, send, waves)


def make_parts(sizes, coeff, offsets, row_table, spectra, keep, send, waves):
    window, kept, n_tile, n_beam = sizes
    share = kept // n_beam
    y_in = iota((2 * ROWS, LANES), 0)
    lane = iota((kept, LANES), 1)
    sign = jnp.where(lane < kept, -1.0, 1.0)
    for group in range(coeff.shape[0]):
        first = group * GROUP
        matrix = coeff[group].reshape(2 * GROUP * ROWS, spectra.shape[1])
        for t in range(0, spectra.shape[0], 2):
            pair = jnp.concatenate([spectra[t], spectra[t + 1]], axis=1)
            made = jnp.dot(matrix, pair, preferred_element_type=f32)
            y = t * ROWS
            for p in range(GROUP):
                offset = offsets[first + p : first + p + 1, :]
                starts_here = p % PER_LIST < CAP
                inside = y_in + y >= offset if starts_here else y_in + y < offset
                for c in range(2):
                    spot = (c * GROUP + p) * ROWS
                    value = made[spot : spot + ROWS, :]
                    value = jnp.concatenate([value[:, :LANES], value[:, LANES:]], axis=0)
                    waves[c, p, y : y + 2 * ROWS, :] = jnp.where(inside, value, 0.0).astype(bf16)
        for p in range(0, GROUP, PER_LIST):
            fields = []
            for q in range(p, p + PER_LIST, 2):
                pair = jnp.concatenate(
                    [waves[:, q + h].reshape(2 * window, LANES) for h in range(2)], axis=1
                )
                both = jnp.dot(row_table[...], pair, preferred_element_type=f32)
                for h in range(2):
                    value = both[:, h * LANES : (h + 1) * LANES]
                    fields.append(value[:kept] + times_i(value[kept:]) * sign)
            k = (first + p) // PER_LIST
            for pos in range(n_beam):
                block = jnp.concatenate([f[pos * share : (pos + 1) * share] for f in fields], axis=0).astype(bf16)
                half = n_beam // 2
                if pos < half:
                    keep[pos, k] = block
                else:
                    send[pos - half, k] = block


def result_kernel(sizes, all_beams, *refs):
    window, kept, n_tile, n_beam = sizes
    turn, select = refs[:2]
    blocks = in_order(refs[2 : 2 + n_tile], orders(n_tile)[1])
    out, intensity = refs[2 + n_tile :]
    height = select.shape[0] // BIN
    shape = (2 * LANES, kept // BIN)
    bins = (iota(shape, 0) % kept // BIN == iota(shape, 1)).astype(f32).astype(bf16)
    arrived = jnp.concatenate([block[...] for block in blocks], axis=0)
    field = jnp.dot(select[...], arrived, preferred_element_type=f32)
    field = field * turn[0] + times_i(field) * turn[1]
    intensity[...] = field * field
    summed = intensity[pl.ds(0, height, stride=BIN), :]
    for b in range(1, BIN):
        summed = summed + intensity[pl.ds(b, height, stride=BIN), :]
    high = summed.astype(bf16)
    low = (summed - high.astype(f32)).astype(bf16)
    binned = jnp.dot(jnp.concatenate([high, low], axis=1), bins, preferred_element_type=f32)
    binned = binned * (1.0 / (BIN * BIN * window * window * all_beams))
    each = height // out.shape[0]
    for j in range(out.shape[0]):
        out[j] = binned[j * each : (j + 1) * each]


VMEM = pl.BlockSpec(memory_space=pltpu.VMEM)
HBM = pl.BlockSpec(memory_space=pltpu.HBM)
SMEM = pl.BlockSpec(memory_space=pltpu.SMEM)


def params(mib=16):
    return pltpu.CompilerParams(vmem_limit_bytes=mib * 1024 * 1024)


def swapped(array, axis, by):
    return lax.ppermute(array, axis, [(i, i ^ by) for i in range(lax.axis_size(axis))])


def shifted(arrays, way, order):
    size = lax.axis_size("tile")
    return [
        lax.ppermute(arrays[k], "tile", [(i, (i + way * k) % size) for i in range(size)]) if k else arrays[0]
        for k in order
    ]


def halves(n_tile):
    numbers = list(range(n_tile))[::-1]
    return numbers[: n_tile // 2], numbers[n_tile // 2 :]


def in_order(refs, order):
    return [refs[order.index(k)] for k in range(len(order))]


def per_device(smatrix, beam_table, probes):
    _, beams, window, _ = smatrix.shape
    kept = window // 2
    n_tile = lax.axis_size("tile")
    n_beam = lax.axis_size("beam")
    sizes = (window, kept, n_tile, n_beam)
    share = kept // n_beam
    slots = n_tile * PER_LIST
    count = probes.shape[0]

    probes = probes.T
    lists_order, results_order = orders(n_tile)
    lists = lax.optimization_barrier(shifted([probes] * n_tile, 1, lists_order))
    lists = dict(zip(lists_order, lists))

    turn, select = pl.pallas_call(
        functools.partial(homing_kernel, sizes),
        in_specs=[SMEM],
        out_specs=[VMEM] * 2,
        out_shape=[
            jax.ShapeDtypeStruct((2, count * share, LANES), f32),
            jax.ShapeDtypeStruct((count * share, slots * share), bf16),
        ],
        compiler_params=params(),
        cost_estimate=pl.CostEstimate(flops=1 << 28, bytes_accessed=1 << 20, transcendentals=0),
        name="homing",
    )(probes)
    spectra, row_table, beam_turns = pl.pallas_call(
        functools.partial(spectra_kernel, sizes),
        in_specs=[HBM, HBM],
        out_specs=[VMEM] * 3,
        out_shape=[
            jax.ShapeDtypeStruct((window // ROWS, beams * ROWS, 2 * kept), bf16),
            jax.ShapeDtypeStruct((2 * kept, 2 * window), bf16),
            jax.ShapeDtypeStruct((3, beams * ROWS), f32),
        ],
        scratch_shapes=[
            pltpu.VMEM((2 * window, 2 * kept), bf16),
            pltpu.VMEM(smatrix.shape, bf16),
            pltpu.VMEM(beam_table.shape, f32),
            pltpu.SemaphoreType.DMA((CHUNKS + 1,)),
        ],
        compiler_params=params(48),
        cost_estimate=pl.CostEstimate(
            flops=2 * beams * window * 4 * window * kept, bytes_accessed=smatrix.size * 3, transcendentals=0
        ),
        name="spectra",
    )(
        pltpu.with_memory_space_constraint(smatrix, pltpu.HBM),
        pltpu.with_memory_space_constraint(beam_table, pltpu.HBM),
    )

    earlier, later = halves(n_tile)

    def parts_call(kernel, numbers, operands, more, scratch, name):
        half = jax.ShapeDtypeStruct((n_beam // 2, len(numbers), PER_LIST * share, LANES), bf16)
        return pl.pallas_call(
            functools.partial(kernel, sizes),
            in_specs=[VMEM] * len(operands),
            out_specs=[VMEM] * (2 + len(more)),
            out_shape=[half, half, *more],
            scratch_shapes=[*scratch, pltpu.VMEM((2, GROUP, window, LANES), bf16)],
            compiler_params=params(),
            cost_estimate=pl.CostEstimate(
                flops=2 * len(numbers) * PER_LIST * 2 * ROWS * beams * window * LANES,
                bytes_accessed=4 * 1024 * 1024,
                transcendentals=0,
            ),
            name=name,
        )(*operands)

    coeff_shape = (len(earlier) * PER_LIST // GROUP, 2, GROUP // 2, 2 * ROWS, beams * ROWS)
    keep, send, coeff, offsets = parts_call(
        coefficients_kernel,
        earlier,
        [lists[n] for n in earlier + later] + [beam_turns, row_table, spectra],
        [
            jax.ShapeDtypeStruct(coeff_shape, bf16),
            jax.ShapeDtypeStruct((len(later) * PER_LIST, LANES), i32),
        ],
        [pltpu.VMEM(coeff_shape, bf16)],
        "coefficients",
    )
    halves_made = [
        (earlier, keep, send),
        (later, *parts_call(parts_kernel, later, [coeff, offsets, row_table, spectra], [], [], "parts")),
    ]

    results = {}
    for numbers, keep, send in halves_made:
        by = 1
        while by < n_beam:
            arrived = swapped(send, "beam", by)
            total = (keep.astype(f32) + arrived.astype(f32)).astype(bf16)
            by *= 2
            middle = total.shape[0] // 2
            keep, send = total[:middle], total[middle:]
        results |= {n: total[0, i] for i, n in enumerate(numbers)}
    blocks = shifted(results, -1, results_order)

    return pl.pallas_call(
        functools.partial(result_kernel, sizes, beams * n_beam),
        in_specs=[VMEM] * (2 + n_tile),
        out_specs=VMEM,
        out_shape=jax.ShapeDtypeStruct((count, share // BIN, kept // BIN), f32),
        scratch_shapes=[pltpu.VMEM((count * share, LANES), f32)],
        compiler_params=params(),
        name="result",
    )(turn, select, *blocks)


def solution(mesh):
    in_specs = (
        P(None, ("groups", "beam"), "tile", None),
        P(None, "beam"),
        P(("groups", "tile"), None),
    )
    out_specs = P(("groups", "tile"), "beam", None)
    return jax.shard_map(
        per_device, mesh=mesh, in_specs=in_specs, out_specs=out_specs, check_vma=False
    )
```

```python
import functools
import math

import jax
import jax.numpy as jnp
from jax import lax
from jax.experimental import pallas as pl
from jax.experimental.pallas import tpu as pltpu
from jax.sharding import PartitionSpec as P

IF = 4
BIN = 2
CAP = 2
PER_LIST = 2 * CAP
LANES = 128
GROUP = 8
CHUNKS = 2
ROWS = 8

LISTS_ORDER = (0, 1, 3, 2)
RESULTS_ORDER = (0, 1, 3, 2)


def orders(n_tile):
    if n_tile == 4:
        return LISTS_ORDER, RESULTS_ORDER
    return tuple(range(n_tile)), tuple(range(n_tile))


two_pi = 2.0 * math.pi
f32 = jnp.float32
bf16 = jnp.bfloat16
i32 = jnp.int32


def iota(shape, dim):
    return lax.broadcasted_iota(i32, shape, dim)


def series(square, last):
    total = jnp.full_like(square, (-1.0) ** (last // 2) / math.factorial(last))
    for n in range(last - 2, -1, -2):
        total = total * square + (-1.0) ** (n // 2) / math.factorial(n)
    return total


def cos_sin(turn):
    x = (turn - jnp.floor(turn + 0.5)) * two_pi
    square = x * x
    return series(square, 18), series(square, 19) * x


def angle_of(index, window):
    half = window // 2
    return (two_pi / window) * (jnp.bitwise_and(index + half, window - 1) - half).astype(f32)


def cosine_of(index, window):
    angle = angle_of(index, window)
    return series(angle * angle, 18)


def bit_reversed(number, count):
    bits = count.bit_length() - 1
    return sum(((number >> b) & 1) << (bits - 1 - b) for b in range(bits))


def window_start(row, window, field_rows):
    start = jnp.right_shift(row, 2) - window // 2
    start = jnp.where(start < 0, start + field_rows, start)
    tile = jnp.right_shift(start, window.bit_length() - 1)
    return tile, jnp.bitwise_and(start, window - 1)


def times_i(pairs):
    return pltpu.roll(pairs, LANES // 2, pairs.ndim - 1)


def spectra_kernel(
    sizes, smatrix_hbm, table_hbm, spectra, row_table, beam_turns, *scratch
):
    window, kept, n_tile, n_beam = sizes
    share = kept // n_beam
    me_beam = lax.axis_index("beam")
    column_table, smatrix, beam_table, sems = scratch
    planes = smatrix.shape[1] // CHUNKS

    def arrival(i):
        chunk = pl.ds(i * planes, planes)
        return pltpu.make_async_copy(smatrix_hbm.at[:, chunk], smatrix.at[:, chunk], sems.at[i])

    for i in range(CHUNKS):
        arrival(i).start()
    tabled = pltpu.make_async_copy(table_hbm, beam_table, sems.at[CHUNKS])
    tabled.start()

    shape = (2 * window, 2 * kept)
    x, part_in = iota(shape, 0) % window, iota(shape, 0) // window
    lane = iota(shape, 1)
    v, part_out = lane % kept - kept // 2, lane // kept
    index = x * v + (window // 4) * (part_out - part_in)
    column_table[...] = cosine_of(index, window).astype(bf16)

    def transform(i, carry):
        arrival(i).wait()
        chunk = pl.ds(i * planes, planes)
        flat = jnp.concatenate([smatrix[c, chunk].reshape(planes * window, window) for c in range(2)], axis=1)
        product = jnp.dot(flat, column_table[...], preferred_element_type=f32)
        product = product.reshape(planes, window // ROWS, ROWS, 2 * kept)
        rows = pl.ds(pl.multiple_of(i * planes * ROWS, planes * ROWS), planes * ROWS)
        for t in range(window // ROWS):
            spectra[t, rows, :] = product[:, t].reshape(planes * ROWS, 2 * kept).astype(bf16)
        return carry

    lax.fori_loop(0, CHUNKS, transform, 0)

    shape = (2 * kept, 2 * window)
    line, turned = iota(shape, 0) % kept, iota(shape, 0) // kept
    r, part_in = iota(shape, 1) % window, iota(shape, 1) // window
    block = line // share
    owner = jnp.zeros_like(block)
    for pos in range(n_beam):
        owner = jnp.where(block == pos, jnp.bitwise_xor(me_beam, bit_reversed(pos, n_beam)), owner)
    u = owner * share + line % share - kept // 2
    index = u * r + (window // 4) * (turned - part_in)
    row_table[...] = cosine_of(index, window).astype(bf16)

    tabled.wait()
    beams, wide = beam_table.shape[1], beam_turns.shape[1]
    spread = (iota((beams, wide), 1) // ROWS == iota((beams, wide), 0)).astype(f32)
    wave_numbers = beam_table[...]
    scale = jnp.where(iota(wave_numbers.shape, 0) < 2, 1.0 / (window * IF), 1.0 / two_pi)
    beam_turns[...] = jnp.dot(
        wave_numbers * scale, spread, precision=lax.Precision.HIGHEST, preferred_element_type=f32
    )


def homing_kernel(sizes, probes, turn, select, bins):
    window, kept, n_tile, n_beam = sizes
    share = kept // n_beam
    me_beam = lax.axis_index("beam")
    me_tile = lax.axis_index("tile")
    each = share // BIN
    height = select.shape[0] // BIN
    u = iota((each, LANES), 0) * BIN + me_beam * share - kept // 2
    lane = iota((each, LANES), 1)
    v = lane % kept - kept // 2
    shape = (select.shape[0], select.shape[1])
    line = iota(shape, 0)
    window_of, slot_of = line % height // each, iota(shape, 1) // share
    wanted = (slot_of == -1, slot_of == -1)
    tiles = []
    for j in range(probes.shape[1]):
        tile, offset = window_start(probes[0, j], window, window * n_tile)
        following = jnp.where(tile == n_tile - 1, 0, tile + 1)
        rank = sum([(t == tile).astype(i32) for t in tiles], i32(0))
        tiles.append(tile)
        spots = [
            (jnp.where(t < me_tile, t + n_tile, t) - me_tile) * PER_LIST + base + rank
            for t, base in ((tile, 0), (following, CAP))
        ]
        wanted = [w | ((window_of == j) & (slot_of == spot)) for w, spot in zip(wanted, spots)]
        shift = jnp.right_shift(probes[1, j], 2) - window // 2
        for b in range(BIN):
            angle = angle_of((u + b) * offset + v * shift, window)
            square = angle * angle
            place = slice(b * height + j * each, b * height + (j + 1) * each)
            turn[0, place, :] = series(square, 18)
            turn[1, place, :] = series(square, 19) * jnp.where(lane < kept, -angle, angle)
    same_line = line % height % each * BIN + line // height == iota(shape, 1) % share
    spread = (iota(bins.shape, 0) % kept // BIN == iota(bins.shape, 1)).astype(f32)
    bins[...] = spread.astype(bf16)
    select[...] = jnp.where((wanted[0] | wanted[1]) & same_line, 1.0, 0.0).astype(bf16)


def chosen(lists, me_tile, window, n_tile):
    shape = (len(lists) * PER_LIST, lists[0].shape[1])
    slot, item = iota(shape, 0), iota(shape, 1)
    rows = jnp.zeros(shape, i32)
    columns = jnp.zeros(shape, i32)
    for n, probes in enumerate(lists):
        here = slot // PER_LIST == n
        rows = jnp.where(here, probes[0:1, :], rows)
        columns = jnp.where(here, probes[1:2, :], columns)
    tile, _ = window_start(rows, window, window * n_tile)
    before = jnp.where(me_tile == 0, n_tile - 1, me_tile - 1)
    match = tile == jnp.where(slot % PER_LIST < CAP, me_tile, before)
    sign = jnp.where(slot % CAP == 0, 1, -1)
    nothing = float(1 << 23)
    found = []
    for values, limit in ((rows, window * n_tile * IF), (columns, window * IF)):
        keys = (sign * (item * limit + values)).astype(f32)
        key = jnp.abs(jnp.min(jnp.where(match, keys, nothing), axis=1, keepdims=True))
        found.append(jnp.bitwise_and(key.astype(i32), limit - 1))
    return found


def coefficients_kernel(sizes, *refs):
    window, kept, n_tile, n_beam = sizes
    lists, (beam_turns, row_table, spectra, keep, send, later, later_offsets, coeff, waves) = refs[:-9], refs[-9:]
    slots = len(lists) * PER_LIST
    wide = beam_turns.shape[1]
    now = keep.shape[1] * PER_LIST
    me_tile = lax.axis_index("tile")
    row_v, column_v = chosen(lists, me_tile, window, n_tile)
    offsets = jnp.bitwise_and(jnp.right_shift(row_v, 2) - window // 2, window - 1)
    offsets = jnp.broadcast_to(offsets, (slots, LANES))
    later_offsets[...] = offsets[now:]
    alpha_re, alpha_im = cos_sin(
        beam_turns[2:3, :] + (beam_turns[0:1, :] * row_v.astype(f32) + beam_turns[1:2, :] * column_v.astype(f32))
    )
    pair = iota((2 * ROWS, wide), 0)
    own_row = iota((2 * ROWS, wide), 1) % ROWS == pair % ROWS
    for c, alpha in enumerate((alpha_re, -alpha_im)):
        for p in range(0, slots, 2):
            lines = jnp.where(pair < ROWS, alpha[p : p + 1, :], alpha[p + 1 : p + 2, :])
            lines = jnp.where(own_row, lines, 0.0).astype(bf16)
            if p < now:
                coeff[p // GROUP, c, p % GROUP // 2] = lines
            else:
                later[(p - now) // GROUP, c, (p - now) % GROUP // 2] = lines
    make_parts(sizes, coeff, offsets[:now], row_table, spectra, keep, send, waves)


def parts_kernel(sizes, coeff, offsets, row_table, spectra, keep, send, waves):
    make_parts(sizes, coeff, offsets[...], row_table, spectra, keep, send, waves)


def make_parts(sizes, coeff, offsets, row_table, spectra, keep, send, waves):
    window, kept, n_tile, n_beam = sizes
    share = kept // n_beam
    y_in = iota((2 * ROWS, LANES), 0)
    lane = iota((kept, LANES), 1)
    sign = jnp.where(lane < kept, -1.0, 1.0)
    for group in range(coeff.shape[0]):
        first = group * GROUP
        matrix = coeff[group].reshape(2 * GROUP * ROWS, spectra.shape[1])
        for t in range(0, spectra.shape[0], 2):
            pair = jnp.concatenate([spectra[t], spectra[t + 1]], axis=1)
            made = jnp.dot(matrix, pair, preferred_element_type=f32)
            y = t * ROWS
            for p in range(GROUP):
                offset = offsets[first + p : first + p + 1, :]
                starts_here = p % PER_LIST < CAP
                inside = y_in + y >= offset if starts_here else y_in + y < offset
                for c in range(2):
                    spot = (c * GROUP + p) * ROWS
                    value = made[spot : spot + ROWS, :]
                    value = jnp.concatenate([value[:, :LANES], value[:, LANES:]], axis=0)
                    waves[c, p, y : y + 2 * ROWS, :] = jnp.where(inside, value, 0.0).astype(bf16)
        for p in range(0, GROUP, PER_LIST):
            fields = []
            for q in range(p, p + PER_LIST, 2):
                pair = jnp.concatenate(
                    [waves[:, q + h].reshape(2 * window, LANES) for h in range(2)], axis=1
                )
                both = jnp.dot(row_table[...], pair, preferred_element_type=f32)
                for h in range(2):
                    value = both[:, h * LANES : (h + 1) * LANES]
                    fields.append(value[:kept] + times_i(value[kept:]) * sign)
            k = (first + p) // PER_LIST
            for pos in range(n_beam):
                block = jnp.concatenate([f[pos * share : (pos + 1) * share] for f in fields], axis=0).astype(bf16)
                half = n_beam // 2
                if pos < half:
                    keep[pos, k] = block
                else:
                    send[pos - half, k] = block


def result_kernel(sizes, all_beams, *refs):
    window, kept, n_tile, n_beam = sizes
    turn, select, bins = refs[:3]
    blocks = in_order(refs[3 : 3 + n_tile], orders(n_tile)[1])
    out = refs[3 + n_tile]
    height = select.shape[0] // BIN
    arrived = jnp.concatenate([block[...] for block in blocks], axis=0)
    field = jnp.dot(select[...], arrived, preferred_element_type=f32)
    field = field * turn[0] + times_i(field) * turn[1]
    intensity = field * field
    summed = sum([intensity[b * height : (b + 1) * height] for b in range(1, BIN)], intensity[:height])
    high = summed.astype(bf16)
    low = (summed - high.astype(f32)).astype(bf16)
    binned = jnp.dot(jnp.concatenate([high, low], axis=1), bins[...], preferred_element_type=f32)
    binned = binned * (1.0 / (BIN * BIN * window * window * all_beams))
    each = height // out.shape[0]
    for j in range(out.shape[0]):
        out[j] = binned[j * each : (j + 1) * each]


VMEM = pl.BlockSpec(memory_space=pltpu.VMEM)
HBM = pl.BlockSpec(memory_space=pltpu.HBM)
SMEM = pl.BlockSpec(memory_space=pltpu.SMEM)


def params(mib=16):
    return pltpu.CompilerParams(vmem_limit_bytes=mib * 1024 * 1024)


def swapped(array, axis, by):
    return lax.ppermute(array, axis, [(i, i ^ by) for i in range(lax.axis_size(axis))])


def shifted(arrays, way, order):
    size = lax.axis_size("tile")
    return [
        lax.ppermute(arrays[k], "tile", [(i, (i + way * k) % size) for i in range(size)]) if k else arrays[0]
        for k in order
    ]


def halves(n_tile):
    numbers = list(range(n_tile))[::-1]
    return numbers[: n_tile // 2], numbers[n_tile // 2 :]


def in_order(refs, order):
    return [refs[order.index(k)] for k in range(len(order))]


def per_device(smatrix, beam_table, probes):
    _, beams, window, _ = smatrix.shape
    kept = window // 2
    n_tile = lax.axis_size("tile")
    n_beam = lax.axis_size("beam")
    sizes = (window, kept, n_tile, n_beam)
    share = kept // n_beam
    slots = n_tile * PER_LIST
    count = probes.shape[0]

    probes = probes.T
    lists_order, results_order = orders(n_tile)
    lists = lax.optimization_barrier(shifted([probes] * n_tile, 1, lists_order))
    lists = dict(zip(lists_order, lists))

    turn, select, bins = pl.pallas_call(
        functools.partial(homing_kernel, sizes),
        in_specs=[SMEM],
        out_specs=[VMEM] * 3,
        out_shape=[
            jax.ShapeDtypeStruct((2, count * share, LANES), f32),
            jax.ShapeDtypeStruct((count * share, slots * share), bf16),
            jax.ShapeDtypeStruct((2 * LANES, kept // BIN), bf16),
        ],
        compiler_params=params(),
        cost_estimate=pl.CostEstimate(flops=1 << 28, bytes_accessed=1 << 20, transcendentals=0),
        name="homing",
    )(probes)
    spectra, row_table, beam_turns = pl.pallas_call(
        functools.partial(spectra_kernel, sizes),
        in_specs=[HBM, HBM],
        out_specs=[VMEM] * 3,
        out_shape=[
            jax.ShapeDtypeStruct((window // ROWS, beams * ROWS, 2 * kept), bf16),
            jax.ShapeDtypeStruct((2 * kept, 2 * window), bf16),
            jax.ShapeDtypeStruct((3, beams * ROWS), f32),
        ],
        scratch_shapes=[
            pltpu.VMEM((2 * window, 2 * kept), bf16),
            pltpu.VMEM(smatrix.shape, bf16),
            pltpu.VMEM(beam_table.shape, f32),
            pltpu.SemaphoreType.DMA((CHUNKS + 1,)),
        ],
        compiler_params=params(48),
        cost_estimate=pl.CostEstimate(
            flops=2 * beams * window * 4 * window * kept, bytes_accessed=smatrix.size * 3, transcendentals=0
        ),
        name="spectra",
    )(
        pltpu.with_memory_space_constraint(smatrix, pltpu.HBM),
        pltpu.with_memory_space_constraint(beam_table, pltpu.HBM),
    )

    earlier, later = halves(n_tile)

    def parts_call(kernel, numbers, operands, more, scratch, name):
        half = jax.ShapeDtypeStruct((n_beam // 2, len(numbers), PER_LIST * share, LANES), bf16)
        return pl.pallas_call(
            functools.partial(kernel, sizes),
            in_specs=[VMEM] * len(operands),
            out_specs=[VMEM] * (2 + len(more)),
            out_shape=[half, half, *more],
            scratch_shapes=[*scratch, pltpu.VMEM((2, GROUP, window, LANES), bf16)],
            compiler_params=params(),
            cost_estimate=pl.CostEstimate(
                flops=2 * len(numbers) * PER_LIST * 2 * ROWS * beams * window * LANES,
                bytes_accessed=4 * 1024 * 1024,
                transcendentals=0,
            ),
            name=name,
        )(*operands)

    coeff_shape = (len(earlier) * PER_LIST // GROUP, 2, GROUP // 2, 2 * ROWS, beams * ROWS)
    keep, send, coeff, offsets = parts_call(
        coefficients_kernel,
        earlier,
        [lists[n] for n in earlier + later] + [beam_turns, row_table, spectra],
        [
            jax.ShapeDtypeStruct(coeff_shape, bf16),
            jax.ShapeDtypeStruct((len(later) * PER_LIST, LANES), i32),
        ],
        [pltpu.VMEM(coeff_shape, bf16)],
        "coefficients",
    )
    halves_made = [
        (earlier, keep, send),
        (later, *parts_call(parts_kernel, later, [coeff, offsets, row_table, spectra], [], [], "parts")),
    ]

    results = {}
    for numbers, keep, send in halves_made:
        by = 1
        while by < n_beam:
            arrived = swapped(send, "beam", by)
            total = (keep.astype(f32) + arrived.astype(f32)).astype(bf16)
            by *= 2
            middle = total.shape[0] // 2
            keep, send = total[:middle], total[middle:]
        results |= {n: total[0, i] for i, n in enumerate(numbers)}
    blocks = shifted(results, -1, results_order)

    return pl.pallas_call(
        functools.partial(result_kernel, sizes, beams * n_beam),
        in_specs=[VMEM] * (3 + n_tile),
        out_specs=VMEM,
        out_shape=jax.ShapeDtypeStruct((count, share // BIN, kept // BIN), f32),
        compiler_params=params(),
        name="result",
    )(turn, select, bins, *blocks)


def solution(mesh):
    in_specs = (
        P(None, ("groups", "beam"), "tile", None),
        P(None, "beam"),
        P(("groups", "tile"), None),
    )
    out_specs = P(("groups", "tile"), "beam", None)
    return jax.shard_map(
        per_device, mesh=mesh, in_specs=in_specs, out_specs=out_specs, check_vma=False
    )
```

```python
import functools
import math

import jax
import jax.numpy as jnp
from jax import lax
from jax.experimental import pallas as pl
from jax.experimental.pallas import tpu as pltpu
from jax.sharding import PartitionSpec as P

IF = 4
BIN = 2
CAP = 2
PER_LIST = 2 * CAP
LANES = 128
GROUP = 8
CHUNKS = 4
ROWS = 8

LISTS_ORDER = (0, 1, 3, 2)
RESULTS_ORDER = (0, 1, 3, 2)


def orders(n_tile):
    if n_tile == 4:
        return LISTS_ORDER, RESULTS_ORDER
    return tuple(range(n_tile)), tuple(range(n_tile))


two_pi = 2.0 * math.pi
f32 = jnp.float32
bf16 = jnp.bfloat16
i32 = jnp.int32


def iota(shape, dim):
    return lax.broadcasted_iota(i32, shape, dim)


def series(square, last):
    total = jnp.full_like(square, (-1.0) ** (last // 2) / math.factorial(last))
    for n in range(last - 2, -1, -2):
        total = total * square + (-1.0) ** (n // 2) / math.factorial(n)
    return total


def cos_sin(turn):
    x = (turn - jnp.floor(turn + 0.5)) * two_pi
    square = x * x
    return series(square, 18), series(square, 19) * x


def angle_of(index, window):
    half = window // 2
    return (two_pi / window) * (jnp.bitwise_and(index + half, window - 1) - half).astype(f32)


def cosine_of(index, window):
    angle = angle_of(index, window)
    return series(angle * angle, 18)


def bit_reversed(number, count):
    bits = count.bit_length() - 1
    return sum(((number >> b) & 1) << (bits - 1 - b) for b in range(bits))


def window_start(row, window, field_rows):
    start = jnp.right_shift(row, 2) - window // 2
    start = jnp.where(start < 0, start + field_rows, start)
    tile = jnp.right_shift(start, window.bit_length() - 1)
    return tile, jnp.bitwise_and(start, window - 1)


def times_i(pairs):
    return pltpu.roll(pairs, LANES // 2, pairs.ndim - 1)


def spectra_kernel(
    sizes, smatrix_hbm, table_hbm, spectra, row_table, beam_turns, *scratch
):
    window, kept, n_tile, n_beam = sizes
    share = kept // n_beam
    me_beam = lax.axis_index("beam")
    column_table, smatrix, beam_table, sems = scratch
    planes = smatrix.shape[1] // CHUNKS

    def arrival(i):
        chunk = pl.ds(i * planes, planes)
        return pltpu.make_async_copy(smatrix_hbm.at[:, chunk], smatrix.at[:, chunk], sems.at[i])

    for i in range(CHUNKS):
        arrival(i).start()
    tabled = pltpu.make_async_copy(table_hbm, beam_table, sems.at[CHUNKS])
    tabled.start()

    shape = (2 * window, 2 * kept)
    x, part_in = iota(shape, 0) % window, iota(shape, 0) // window
    lane = iota(shape, 1)
    v, part_out = lane % kept - kept // 2, lane // kept
    index = x * v + (window // 4) * (part_out - part_in)
    column_table[...] = cosine_of(index, window).astype(bf16)

    def transform(i, carry):
        arrival(i).wait()
        chunk = pl.ds(i * planes, planes)
        flat = jnp.concatenate([smatrix[c, chunk].reshape(planes * window, window) for c in range(2)], axis=1)
        product = jnp.dot(flat, column_table[...], preferred_element_type=f32)
        product = product.reshape(planes, window // ROWS, ROWS, 2 * kept)
        rows = pl.ds(pl.multiple_of(i * planes * ROWS, planes * ROWS), planes * ROWS)
        for t in range(window // ROWS):
            spectra[t, rows, :] = product[:, t].reshape(planes * ROWS, 2 * kept).astype(bf16)
        return carry

    lax.fori_loop(0, CHUNKS, transform, 0)

    shape = (2 * kept, 2 * window)
    line, turned = iota(shape, 0) % kept, iota(shape, 0) // kept
    r, part_in = iota(shape, 1) % window, iota(shape, 1) // window
    block = line // share
    owner = jnp.zeros_like(block)
    for pos in range(n_beam):
        owner = jnp.where(block == pos, jnp.bitwise_xor(me_beam, bit_reversed(pos, n_beam)), owner)
    u = owner * share + line % share - kept // 2
    index = u * r + (window // 4) * (turned - part_in)
    row_table[...] = cosine_of(index, window).astype(bf16)

    tabled.wait()
    beams, wide = beam_table.shape[1], beam_turns.shape[1]
    spread = (iota((beams, wide), 1) // ROWS == iota((beams, wide), 0)).astype(f32)
    wave_numbers = beam_table[...]
    scale = jnp.where(iota(wave_numbers.shape, 0) < 2, 1.0 / (window * IF), 1.0 / two_pi)
    beam_turns[...] = jnp.dot(
        wave_numbers * scale, spread, precision=lax.Precision.HIGHEST, preferred_element_type=f32
    )


def homing_kernel(sizes, probes, turn, select):
    window, kept, n_tile, n_beam = sizes
    share = kept // n_beam
    me_beam = lax.axis_index("beam")
    me_tile = lax.axis_index("tile")
    u = iota((share, LANES), 0) + me_beam * share - kept // 2
    lane = iota((share, LANES), 1)
    v = lane % kept - kept // 2
    shape = (select.shape[0], select.shape[1])
    window_of, slot_of = iota(shape, 0) // share, iota(shape, 1) // share
    wanted = (slot_of == -1, slot_of == -1)
    tiles = []
    for j in range(probes.shape[1]):
        tile, offset = window_start(probes[0, j], window, window * n_tile)
        following = jnp.where(tile == n_tile - 1, 0, tile + 1)
        rank = sum([(t == tile).astype(i32) for t in tiles], i32(0))
        tiles.append(tile)
        spots = [
            (jnp.where(t < me_tile, t + n_tile, t) - me_tile) * PER_LIST + base + rank
            for t, base in ((tile, 0), (following, CAP))
        ]
        wanted = [w | ((window_of == j) & (slot_of == spot)) for w, spot in zip(wanted, spots)]
        shift = jnp.right_shift(probes[1, j], 2) - window // 2
        angle = angle_of(u * offset + v * shift, window)
        square = angle * angle
        turn[0, j * share : (j + 1) * share, :] = series(square, 18)
        turn[1, j * share : (j + 1) * share, :] = series(square, 19) * jnp.where(lane < kept, -angle, angle)
    same_line = iota(shape, 0) % share == iota(shape, 1) % share
    select[...] = jnp.where((wanted[0] | wanted[1]) & same_line, 1.0, 0.0).astype(bf16)


def chosen(lists, me_tile, window, n_tile):
    shape = (len(lists) * PER_LIST, lists[0].shape[1])
    slot, item = iota(shape, 0), iota(shape, 1)
    rows = jnp.zeros(shape, i32)
    columns = jnp.zeros(shape, i32)
    for n, probes in enumerate(lists):
        here = slot // PER_LIST == n
        rows = jnp.where(here, probes[0:1, :], rows)
        columns = jnp.where(here, probes[1:2, :], columns)
    tile, _ = window_start(rows, window, window * n_tile)
    before = jnp.where(me_tile == 0, n_tile - 1, me_tile - 1)
    match = tile == jnp.where(slot % PER_LIST < CAP, me_tile, before)
    sign = jnp.where(slot % CAP == 0, 1, -1)
    nothing = float(1 << 23)
    found = []
    for values, limit in ((rows, window * n_tile * IF), (columns, window * IF)):
        keys = (sign * (item * limit + values)).astype(f32)
        key = jnp.abs(jnp.min(jnp.where(match, keys, nothing), axis=1, keepdims=True))
        found.append(jnp.bitwise_and(key.astype(i32), limit - 1))
    return found


def coefficients_kernel(sizes, *refs):
    window, kept, n_tile, n_beam = sizes
    lists, (beam_turns, row_table, spectra, keep, send, later, later_offsets, coeff, waves) = refs[:-9], refs[-9:]
    slots = len(lists) * PER_LIST
    wide = beam_turns.shape[1]
    now = keep.shape[1] * PER_LIST
    me_tile = lax.axis_index("tile")
    row_v, column_v = chosen(lists, me_tile, window, n_tile)
    offsets = jnp.bitwise_and(jnp.right_shift(row_v, 2) - window // 2, window - 1)
    offsets = jnp.broadcast_to(offsets, (slots, LANES))
    later_offsets[...] = offsets[now:]
    alpha_re, alpha_im = cos_sin(
        beam_turns[2:3, :] + (beam_turns[0:1, :] * row_v.astype(f32) + beam_turns[1:2, :] * column_v.astype(f32))
    )
    pair = iota((2 * ROWS, wide), 0)
    own_row = iota((2 * ROWS, wide), 1) % ROWS == pair % ROWS
    for c, alpha in enumerate((alpha_re, -alpha_im)):
        for p in range(0, slots, 2):
            lines = jnp.where(pair < ROWS, alpha[p : p + 1, :], alpha[p + 1 : p + 2, :])
            lines = jnp.where(own_row, lines, 0.0).astype(bf16)
            if p < now:
                coeff[p // GROUP, c, p % GROUP // 2] = lines
            else:
                later[(p - now) // GROUP, c, (p - now) % GROUP // 2] = lines
    make_parts(sizes, coeff, offsets[:now], row_table, spectra, keep, send, waves)


def parts_kernel(sizes, coeff, offsets, row_table, spectra, keep, send, waves):
    make_parts(sizes, coeff, offsets[...], row_table, spectra, keep, send, waves)


def make_parts(sizes, coeff, offsets, row_table, spectra, keep, send, waves):
    window, kept, n_tile, n_beam = sizes
    share = kept // n_beam
    y_in = iota((2 * ROWS, LANES), 0)
    lane = iota((kept, LANES), 1)
    sign = jnp.where(lane < kept, -1.0, 1.0)
    for group in range(coeff.shape[0]):
        first = group * GROUP
        matrix = coeff[group].reshape(2 * GROUP * ROWS, spectra.shape[1])
        for t in range(0, spectra.shape[0], 2):
            pair = jnp.concatenate([spectra[t], spectra[t + 1]], axis=1)
            made = jnp.dot(matrix, pair, preferred_element_type=f32)
            y = t * ROWS
            for p in range(GROUP):
                offset = offsets[first + p : first + p + 1, :]
                starts_here = p % PER_LIST < CAP
                inside = y_in + y >= offset if starts_here else y_in + y < offset
                for c in range(2):
                    spot = (c * GROUP + p) * ROWS
                    value = made[spot : spot + ROWS, :]
                    value = jnp.concatenate([value[:, :LANES], value[:, LANES:]], axis=0)
                    waves[c, p, y : y + 2 * ROWS, :] = jnp.where(inside, value, 0.0).astype(bf16)
        for p in range(0, GROUP, PER_LIST):
            fields = []
            for q in range(p, p + PER_LIST, 2):
                pair = jnp.concatenate(
                    [waves[:, q + h].reshape(2 * window, LANES) for h in range(2)], axis=1
                )
                both = jnp.dot(row_table[...], pair, preferred_element_type=f32)
                for h in range(2):
                    value = both[:, h * LANES : (h + 1) * LANES]
                    fields.append(value[:kept] + times_i(value[kept:]) * sign)
            k = (first + p) // PER_LIST
            for pos in range(n_beam):
                block = jnp.concatenate([f[pos * share : (pos + 1) * share] for f in fields], axis=0).astype(bf16)
                half = n_beam // 2
                if pos < half:
                    keep[pos, k] = block
                else:
                    send[pos - half, k] = block


def result_kernel(sizes, all_beams, *refs):
    window, kept, n_tile, n_beam = sizes
    turn, select = refs[:2]
    blocks = in_order(refs[2 : 2 + n_tile], orders(n_tile)[1])
    out, intensity = refs[2 + n_tile :]
    height = select.shape[0] // BIN
    shape = (2 * LANES, kept // BIN)
    bins = (iota(shape, 0) % kept // BIN == iota(shape, 1)).astype(f32).astype(bf16)
    arrived = jnp.concatenate([block[...] for block in blocks], axis=0)
    field = jnp.dot(select[...], arrived, preferred_element_type=f32)
    field = field * turn[0] + times_i(field) * turn[1]
    intensity[...] = field * field
    summed = intensity[pl.ds(0, height, stride=BIN), :]
    for b in range(1, BIN):
        summed = summed + intensity[pl.ds(b, height, stride=BIN), :]
    high = summed.astype(bf16)
    low = (summed - high.astype(f32)).astype(bf16)
    binned = jnp.dot(jnp.concatenate([high, low], axis=1), bins, preferred_element_type=f32)
    binned = binned * (1.0 / (BIN * BIN * window * window * all_beams))
    each = height // out.shape[0]
    for j in range(out.shape[0]):
        out[j] = binned[j * each : (j + 1) * each]


VMEM = pl.BlockSpec(memory_space=pltpu.VMEM)
HBM = pl.BlockSpec(memory_space=pltpu.HBM)
SMEM = pl.BlockSpec(memory_space=pltpu.SMEM)


def params(mib=16):
    return pltpu.CompilerParams(vmem_limit_bytes=mib * 1024 * 1024)


def swapped(array, axis, by):
    return lax.ppermute(array, axis, [(i, i ^ by) for i in range(lax.axis_size(axis))])


def shifted(arrays, way, order):
    size = lax.axis_size("tile")
    return [
        lax.ppermute(arrays[k], "tile", [(i, (i + way * k) % size) for i in range(size)]) if k else arrays[0]
        for k in order
    ]


def halves(n_tile):
    numbers = list(range(n_tile))[::-1]
    return numbers[: n_tile // 2], numbers[n_tile // 2 :]


def in_order(refs, order):
    return [refs[order.index(k)] for k in range(len(order))]


def per_device(smatrix, beam_table, probes):
    _, beams, window, _ = smatrix.shape
    kept = window // 2
    n_tile = lax.axis_size("tile")
    n_beam = lax.axis_size("beam")
    sizes = (window, kept, n_tile, n_beam)
    share = kept // n_beam
    slots = n_tile * PER_LIST
    count = probes.shape[0]

    probes = probes.T
    lists_order, results_order = orders(n_tile)
    lists = lax.optimization_barrier(shifted([probes] * n_tile, 1, lists_order))
    lists = dict(zip(lists_order, lists))

    turn, select = pl.pallas_call(
        functools.partial(homing_kernel, sizes),
        in_specs=[SMEM],
        out_specs=[VMEM] * 2,
        out_shape=[
            jax.ShapeDtypeStruct((2, count * share, LANES), f32),
            jax.ShapeDtypeStruct((count * share, slots * share), bf16),
        ],
        compiler_params=params(),
        cost_estimate=pl.CostEstimate(flops=1 << 28, bytes_accessed=1 << 20, transcendentals=0),
        name="homing",
    )(probes)
    spectra, row_table, beam_turns = pl.pallas_call(
        functools.partial(spectra_kernel, sizes),
        in_specs=[HBM, HBM],
        out_specs=[VMEM] * 3,
        out_shape=[
            jax.ShapeDtypeStruct((window // ROWS, beams * ROWS, 2 * kept), bf16),
            jax.ShapeDtypeStruct((2 * kept, 2 * window), bf16),
            jax.ShapeDtypeStruct((3, beams * ROWS), f32),
        ],
        scratch_shapes=[
            pltpu.VMEM((2 * window, 2 * kept), bf16),
            pltpu.VMEM(smatrix.shape, bf16),
            pltpu.VMEM(beam_table.shape, f32),
            pltpu.SemaphoreType.DMA((CHUNKS + 1,)),
        ],
        compiler_params=params(48),
        cost_estimate=pl.CostEstimate(
            flops=2 * beams * window * 4 * window * kept, bytes_accessed=smatrix.size * 3, transcendentals=0
        ),
        name="spectra",
    )(
        pltpu.with_memory_space_constraint(smatrix, pltpu.HBM),
        pltpu.with_memory_space_constraint(beam_table, pltpu.HBM),
    )

    earlier, later = halves(n_tile)

    def parts_call(kernel, numbers, operands, more, scratch, name):
        half = jax.ShapeDtypeStruct((n_beam // 2, len(numbers), PER_LIST * share, LANES), bf16)
        return pl.pallas_call(
            functools.partial(kernel, sizes),
            in_specs=[VMEM] * len(operands),
            out_specs=[VMEM] * (2 + len(more)),
            out_shape=[half, half, *more],
            scratch_shapes=[*scratch, pltpu.VMEM((2, GROUP, window, LANES), bf16)],
            compiler_params=params(),
            cost_estimate=pl.CostEstimate(
                flops=2 * len(numbers) * PER_LIST * 2 * ROWS * beams * window * LANES,
                bytes_accessed=4 * 1024 * 1024,
                transcendentals=0,
            ),
            name=name,
        )(*operands)

    coeff_shape = (len(earlier) * PER_LIST // GROUP, 2, GROUP // 2, 2 * ROWS, beams * ROWS)
    keep, send, coeff, offsets = parts_call(
        coefficients_kernel,
        earlier,
        [lists[n] for n in earlier + later] + [beam_turns, row_table, spectra],
        [
            jax.ShapeDtypeStruct(coeff_shape, bf16),
            jax.ShapeDtypeStruct((len(later) * PER_LIST, LANES), i32),
        ],
        [pltpu.VMEM(coeff_shape, bf16)],
        "coefficients",
    )
    halves_made = [
        (earlier, keep, send),
        (later, *parts_call(parts_kernel, later, [coeff, offsets, row_table, spectra], [], [], "parts")),
    ]

    results = {}
    for numbers, keep, send in halves_made:
        by = 1
        while by < n_beam:
            arrived = swapped(send, "beam", by)
            total = (keep.astype(f32) + arrived.astype(f32)).astype(bf16)
            by *= 2
            middle = total.shape[0] // 2
            keep, send = total[:middle], total[middle:]
        results |= {n: total[0, i] for i, n in enumerate(numbers)}
    blocks = shifted(results, -1, results_order)

    return pl.pallas_call(
        functools.partial(result_kernel, sizes, beams * n_beam),
        in_specs=[VMEM] * (2 + n_tile),
        out_specs=VMEM,
        out_shape=jax.ShapeDtypeStruct((count, share // BIN, kept // BIN), f32),
        scratch_shapes=[pltpu.VMEM((count * share, LANES), f32)],
        compiler_params=params(),
        name="result",
    )(turn, select, *blocks)


def solution(mesh):
    in_specs = (
        P(None, ("groups", "beam"), "tile", None),
        P(None, "beam"),
        P(("groups", "tile"), None),
    )
    out_specs = P(("groups", "tile"), "beam", None)
    return jax.shard_map(
        per_device, mesh=mesh, in_specs=in_specs, out_specs=out_specs, check_vma=False
    )
```
